256 devices in a mesh: sub: 32 (over y, z), nar: 8 (over x, core).
Axes of the slice: x: 4, y: 4, z: 8, core: 2. Of those that a mesh axis runs over, the one named last changes fastest.
Arguments:
- residual: float32 [32, 32, 2048], P(None, 'sub', 'nar')
- iterate: float32 [32, 32, 2048], P(None, 'sub', 'nar'), may hold values from -6 to 6
- stiffness: float32 [32, 2048, 3072], P('sub', 'nar')
- local_inverse: float32 [32, 2048, 3072], P('sub', 'nar')
- eigvecs: float32 [32, 96, 2048], P('sub', None, 'nar'), may hold values from -0.125 to 0.125
- ev_count: int32 [32], P('sub'), may hold values from 16 to 96
- coarse_inverse: float32 [3072, 3072], P('sub', 'nar'), may hold values from -0.109375 to 0.109375
- send_rows: int32 [2, 32, 512], P(None, 'sub', 'nar'), may hold values from 0 to 255, as said below
Outputs:
- next_vector: float32 [32, 32, 2048], P(None, 'sub', 'nar')
- new_iterate: float32 [32, 32, 2048], P(None, 'sub', 'nar')
- hessenberg: float32 [3, 32], replicated
The draws below stay inside these ranges and needn't reach their ends.
Inputs may be any that keep to these rules, and one draw needn't show every extreme that they name: `send_rows`: each device's list of 64 rows holds distinct rows of its own block of 256.
All inputs are finite; a program needn't handle non-finite values.
Results may differ from the reference program's by a relative error of at most 0.00015.
Values sent between devices are 32-bit elements; how exact they have to be, the bound alone decides.
No kernel may reach another device: no remote copies, remote signals or barrier semaphores. Data moves between devices by JAX's collectives and lax.ppermute only.
A program may use at most 64 MiB of HBM per device.

```python
import math
import jax
import jax.numpy as jnp
from jax import lax

R_DEV = 256
NRHS = 32
MAXEV = 96
OVD = 64
NSUB = 32
R_SUB = 2048
R_EXT = 3072
NC = 3072
N_NAR = 8


def ramp_values():
    return 1.0 + 2.0 * jnp.arange(NSUB, dtype=jnp.float32) / max(NSUB - 1, 1)


def draw_residual(key, part):
    key = jax.random.fold_in(key, 11)
    first, second = jax.random.split(key)
    shape = (NRHS, NSUB, R_SUB)
    base = jax.random.normal(first, shape, jnp.float32)
    scale = jnp.exp(jax.random.uniform(second, (NRHS, 1, 1), jnp.float32, 0.0, math.log(10.0)))
    return base * ramp_values()[None, :, None] * scale


def banded(key, low, high, ramped):
    first, second = jax.random.split(key, 2)
    noise = jax.random.normal(first, (NSUB, R_SUB, R_EXT), jnp.float32) * (0.5 / math.sqrt(R_EXT))
    diag = (jnp.arange(R_SUB)[:, None] == jnp.arange(R_EXT)[None, :]).astype(jnp.float32)
    modulus = jnp.exp(jax.random.uniform(second, (NSUB, R_SUB, 1), jnp.float32, math.log(low), math.log(high)))
    if ramped:
        modulus = modulus * ramp_values()[:, None, None]
    return modulus * (diag + noise)


def draw_stiffness(key, part):
    key = jax.random.fold_in(key, 12)
    return banded(key, 1.0, 10.0, True)


def draw_local_inverse(key, part):
    key = jax.random.fold_in(key, 13)
    return banded(key, 0.5, 2.0, False)


def draw_ev_count(key, part):
    key = jax.random.fold_in(key, 14)
    first, second = jax.random.split(key)
    counts = jax.random.randint(first, (NSUB,), MAXEV // 6, MAXEV + 1).astype(jnp.int32)
    order = jax.random.permutation(second, NSUB)
    counts = counts.at[order[0]].set(MAXEV)
    return counts.at[order[1]].set(MAXEV // 6)


def one_list(key):
    first, second = jax.random.split(key)
    picked = jax.random.permutation(first, R_DEV - 1)[:OVD - 1].astype(jnp.int32)
    rows = jnp.concatenate([picked, jnp.full((1,), R_DEV - 1, jnp.int32)])
    return rows[jax.random.permutation(second, OVD)]


def draw_send_rows(key, part):
    key = jax.random.fold_in(key, 15)
    keys = jax.random.split(key, 2 * NSUB * N_NAR)
    lists = jax.vmap(one_list)(keys)
    return lists.reshape(2, NSUB, N_NAR * OVD).astype(jnp.int32)


def levels(rng, extent, cuts, smallest, largest):
    loudness, own = 1.0, jax.random.fold_in(rng, 6)
    for dim, shards_of in cuts:
        steps = jnp.exp(jax.random.uniform(jax.random.fold_in(own, dim), (shards_of,), jnp.float32, smallest / len(cuts), largest / len(cuts)))
        loudness = loudness * jnp.repeat(steps, extent[dim] // shards_of).reshape([-1 if axis == dim else 1 for axis in range(len(extent))])
    return loudness


def scatter_about(own_key, extent, spread, limit, cuts=(), kind=jnp.bfloat16):
    gain = levels(own_key, extent, cuts, -0.22, 0.18) if cuts else 1.0
    entries = jax.random.normal(own_key, extent, jnp.float32) * spread * gain
    return jnp.minimum(jnp.maximum(entries, -limit), limit).astype(kind)


def setup_inputs(seed: int = 0) -> dict:
    key_of = jax.random.split(jax.random.key(seed), 9)
    return {
        "residual": draw_residual(jax.random.fold_in(key_of[8], 71), 0),
        "iterate": scatter_about(key_of[1], (NRHS, NSUB, R_SUB), 1.0, 6.0, ((1, 32), (2, 8)), jnp.float32),
        "stiffness": draw_stiffness(jax.random.fold_in(key_of[8], 71), 0),
        "local_inverse": draw_local_inverse(jax.random.fold_in(key_of[8], 71), 0),
        "eigvecs": scatter_about(key_of[4], (NSUB, MAXEV, R_SUB), R_SUB ** -0.5, 0.125, ((0, 32), (2, 8)), jnp.float32),
        "ev_count": draw_ev_count(jax.random.fold_in(key_of[8], 71), 0),
        "coarse_inverse": scatter_about(key_of[6], (NC, NC), NC ** -0.5, 0.109375, ((0, 32), (1, 8)), jnp.float32),
        "send_rows": draw_send_rows(jax.random.fold_in(key_of[8], 71), 0),
    }


EPS = 1e-06

def extend(field, send_rows):
    count, nsub, rsub = field.shape
    n_over = send_rows.shape[2]
    over = n_over // N_NAR
    offsets = (jnp.arange(n_over) // over * (rsub // N_NAR)).astype(jnp.int32)
    rows = (send_rows + offsets[None, None, :]).astype(jnp.int32)
    toward_right = jnp.take_along_axis(field, jnp.broadcast_to(rows[0][None], (count, nsub, n_over)), axis=2)
    toward_left = jnp.take_along_axis(field, jnp.broadcast_to(rows[1][None], (count, nsub, n_over)), axis=2)
    blank = jnp.zeros((count, 1, n_over), jnp.float32)
    from_left = jnp.concatenate([blank, toward_right[:, :-1]], axis=1)
    from_right = jnp.concatenate([toward_left[:, 1:], blank], axis=1)
    return jnp.concatenate([field, from_left, from_right], axis=2)

def precondition(field, local_inverse, eigvecs, ev_count, coarse_inverse, send_rows):
    local = jnp.einsum('sre,kse->ksr', local_inverse, extend(field, send_rows), precision=lax.Precision.HIGHEST)
    live = jnp.arange(MAXEV)[None, :] < ev_count[:, None]
    coarse_res = jnp.einsum('sjr,ksr->ksj', eigvecs, field, precision=lax.Precision.HIGHEST)
    coarse_res = jnp.where(live[None], coarse_res, 0.0)
    flat = coarse_res.reshape(field.shape[0], NC)
    coarse_sol = jnp.einsum('cd,kd->kc', coarse_inverse, flat, precision=lax.Precision.HIGHEST)
    coarse_sol = jnp.where(live[None], coarse_sol.reshape(field.shape[0], NSUB, MAXEV), 0.0)
    return local + jnp.einsum('sjr,ksj->ksr', eigvecs, coarse_sol, precision=lax.Precision.HIGHEST)

def inner(first, second):
    return lax.optimization_barrier(jnp.sum(first * second, axis=(1, 2))) / (NSUB * R_SUB)

def reference(residual, iterate, stiffness, local_inverse, eigvecs, ev_count, coarse_inverse, send_rows):
    beta = jnp.sqrt(inner(residual, residual) + EPS)
    start = residual / beta[:, None, None]
    precond = precondition(start, local_inverse, eigvecs, ev_count, coarse_inverse, send_rows)
    image = jnp.einsum('sre,kse->ksr', stiffness, extend(precond, send_rows), precision=lax.Precision.HIGHEST)
    h00 = inner(start, image)
    remainder = image - h00[:, None, None] * start
    h10 = jnp.sqrt(inner(remainder, remainder) + EPS)
    next_vector = remainder / h10[:, None, None]
    factor = beta * h00 / (h00 * h00 + h10 * h10)
    new_iterate = iterate + factor[:, None, None] * precond
    return (next_vector, new_iterate, jnp.stack([beta, h00, h10]))
```

```python
import jax
import jax.numpy as jnp
from jax import lax
from jax.sharding import PartitionSpec as P

EPS = 1e-06
HIGH = lax.Precision.HIGH
HIGHEST = lax.Precision.HIGHEST


def spread(block, axes, count):
    copies = jnp.broadcast_to(block[None], (count,) + block.shape)
    return lax.all_to_all(copies, axes, 0, 0)


def pair_routes(nsub):
    odd = [(i, i ^ 1) for i in range(nsub)]
    even = [(i, (i + 1 if i % 2 else i - 1) % nsub) for i in range(nsub)]
    return odd, even


def beside(first, second, nsub):
    sub = lax.axis_index("sub")
    route_a, route_b = pair_routes(nsub)
    got_a = lax.ppermute(first, "sub", route_a)
    got_b = lax.ppermute(second, "sub", route_b)
    even = sub % 2 == 0
    lefts = jnp.where(sub == 0, 0.0, jnp.where(even, got_b, got_a))
    rights = jnp.where(sub == nsub - 1, 0.0, jnp.where(even, got_a, got_b))
    return jnp.concatenate([lefts, rights], axis=1)


def in_rows(blocks):
    return jnp.swapaxes(blocks, 0, 1).reshape(blocks.shape[1], -1)


def times(field, matrix, precision=HIGH):
    return lax.dot_general(field, matrix, (((1,), (1,)), ((), ())), precision=precision)


def per_device(
    residual, iterate, stiffness, local_inverse, eigvecs, ev_count, coarse_inverse, send_rows
):
    nsub, nnar = lax.axis_size("sub"), lax.axis_size("nar")
    count, _, rdev = residual.shape
    total = nsub * nnar * rdev
    over = send_rows.shape[2]
    maxev = eigvecs.shape[1]
    per_nar = nsub // nnar
    own = nnar * rdev
    sub, nar = lax.axis_index("sub"), lax.axis_index("nar")

    r = residual[:, 0, :]
    live = jnp.arange(maxev)[:, None] < ev_count[0]
    vecs = jnp.where(live, eigvecs[0], 0.0)
    even = sub % 2 == 0
    rights, lefts = send_rows[0, 0], send_rows[1, 0]
    picked = jnp.concatenate([jnp.where(even, rights, lefts), jnp.where(even, lefts, rights)])
    pick = (jnp.arange(rdev)[:, None] == picked[None, :]).astype(jnp.float32)

    def chosen(field):
        return jnp.dot(field, pick, precision=HIGHEST)

    partial_res = times(r, vecs)
    norm = jnp.sum(r * r, axis=1, keepdims=True)
    tail = jnp.zeros((count, 128 - maxev - 1), jnp.float32)
    block = jnp.concatenate([r, chosen(r), partial_res, norm, tail], axis=1)
    got = spread(block, "nar", nnar)
    res = jnp.sum(got[:, :, rdev + 2 * over :], axis=0)
    r_own = in_rows(got[:, :, :rdev])
    to_a = in_rows(got[:, :, rdev : rdev + over])
    to_b = in_rows(got[:, :, rdev + over : rdev + 2 * over])
    r_margin = beside(to_a, to_b, nsub)
    local = times(r_own, local_inverse[0, :, :own])

    whole = spread(res, "sub", nsub)
    norms = jnp.sum(whole[:, :, maxev], axis=0)
    beta = jnp.sqrt(norms / total + EPS)
    piece = lax.dynamic_slice_in_dim(whole, nar * per_nar, per_nar, 0)[:, :, :maxev]
    sol_part = times(in_rows(piece), coarse_inverse)
    sol = jnp.sum(spread(sol_part, "nar", nnar), axis=0)
    local = local + times(r_margin, local_inverse[0, :, own:])
    correction = jnp.dot(sol, vecs, precision=HIGH)
    precond = (local + correction) / beta[:, None]
    start = r / beta[:, None]

    block = jnp.concatenate([precond, chosen(precond)], axis=1)
    got = spread(block, "nar", nnar)
    p_own = in_rows(got[:, :, :rdev])
    to_a = in_rows(got[:, :, rdev : rdev + over])
    to_b = in_rows(got[:, :, rdev + over :])
    p_margin = beside(to_a, to_b, nsub)
    image = times(p_own, stiffness[0, :, :own]) + times(p_margin, stiffness[0, :, own:])

    n_d = jnp.sum(start * start, axis=1)
    a_d = jnp.sum(start * image, axis=1)

    def ratio(a, n):
        return jnp.where(n > 0, a / jnp.where(n > 0, n, 1.0), 0.0)

    h_d = ratio(a_d, n_d)
    off = image - h_d[:, None] * start
    s_d = jnp.sum(off * off, axis=1)
    stats = jnp.concatenate([n_d, a_d, s_d, jnp.zeros_like(n_d)])[None]
    stats = spread(stats, ("sub", "nar"), nsub * nnar)[:, 0]
    n_i, a_i, s_i = (stats[:, i * count : (i + 1) * count] for i in range(3))
    n, a = jnp.sum(n_i, axis=0), jnp.sum(a_i, axis=0)
    h = ratio(a, n)
    gap = ratio(a_i, n_i) - h[None]
    square = jnp.sum(s_i + (n_i * gap) * gap, axis=0)
    lost = EPS / (beta * beta)
    h00 = a / total
    square = square + a * h * (lost * lost)
    h10 = jnp.sqrt(square / total + EPS)
    remainder = image - h00[:, None] * start
    next_vector = remainder / h10[:, None]
    factor = beta * h00 / (h00 * h00 + h10 * h10)
    new_iterate = iterate[:, 0, :] + factor[:, None] * precond
    return (
        next_vector[:, None, :],
        new_iterate[:, None, :],
        jnp.stack([beta, h00, h10]),
    )


def solution(mesh):
    return jax.shard_map(
        per_device,
        mesh=mesh,
        in_specs=(
            P(None, "sub", "nar"),
            P(None, "sub", "nar"),
            P("sub", "nar", None),
            P("sub", "nar", None),
            P("sub", None, "nar"),
            P("sub"),
            P("sub", "nar"),
            P(None, "sub", "nar"),
        ),
        out_specs=(P(None, "sub", "nar"), P(None, "sub", "nar"), P()),
        check_vma=False,
    )
```

```python
import functools

import jax
import jax.numpy as jnp
from jax import lax
from jax.experimental import pallas as pl
from jax.experimental.pallas import tpu as pltpu
from jax.sharding import PartitionSpec as P

EPS = 1e-06
HIGH = lax.Precision.HIGH
F32, BF16 = jnp.float32, jnp.bfloat16
LANES = 128
NT = (((1,), (1,)), ((), ()))
NN = (((1,), (0,)), ((), ()))


def shape(*dims):
    return jax.ShapeDtypeStruct(dims, F32)


VMEM = pl.BlockSpec(memory_space=pltpu.VMEM)
SMEM = pl.BlockSpec(memory_space=pltpu.SMEM)


def local_call(body, outs, in_specs, *args, scratch=(), **options):
    many = isinstance(outs, tuple)
    return pl.pallas_call(
        body,
        out_shape=outs,
        in_specs=in_specs,
        out_specs=tuple(VMEM for _ in outs) if many else VMEM,
        scratch_shapes=scratch,
        compiler_params=pltpu.CompilerParams(vmem_limit_bytes=32 * 2**20),
        **options,
    )(*args)


def halves(x):
    high = x.astype(BF16)
    return high, (x - high.astype(F32)).astype(BF16)


def dot3(a, b, dims):
    dot = functools.partial(lax.dot_general, dimension_numbers=dims, preferred_element_type=F32)
    (ah, al), (bh, bl) = halves(a), halves(b)
    return dot(ah, bh) + (dot(al, bh) + dot(ah, bl))


def exactly(pick, x, dims, first):
    high = x.astype(BF16)
    rest = x - high.astype(F32)
    mid = rest.astype(BF16)
    low = (rest - mid.astype(F32)).astype(BF16)
    total = None
    for part in (low, mid, high):
        pair = (pick, part) if first else (part, pick)
        term = lax.dot_general(*pair, dimension_numbers=dims, preferred_element_type=F32)
        total = term if total is None else total + term
    return total


def iota(dims, axis):
    return lax.broadcasted_iota(jnp.int32, dims, axis)


def as_row(col):
    k = col.shape[0]
    return jnp.sum(jnp.where(iota((k, LANES), 0) == iota((k, LANES), 1), col, 0.0), axis=0, keepdims=True)


def as_col(row, k):
    return jnp.sum(jnp.where(iota((k, LANES), 0) == iota((k, LANES), 1), row, 0.0), axis=1, keepdims=True)


def picker(rows_ref, rdev):
    even = lax.axis_index("sub") % 2 == 0
    rights, lefts = rows_ref[0], rows_ref[1]
    picked = jnp.concatenate([jnp.where(even, rights, lefts), jnp.where(even, lefts, rights)], axis=1)
    return (iota((rdev, LANES), 0) == picked).astype(F32).astype(BF16)


def masked(vecs_ref, count_ref):
    vecs = vecs_ref[0]
    return jnp.where(iota(vecs.shape, 0) < count_ref[0], vecs, 0.0)


def begin_kernel(res_ref, vecs_ref, count_ref, part_ref, wide_ref):
    k, _, rdev = res_ref.shape
    r = res_ref[:, 0, :]
    vecs = masked(vecs_ref, count_ref)
    ncol = LANES // k
    rows = vecs.shape[0] // ncol
    wide_ref[...] = jnp.zeros_like(wide_ref)
    for b in range(ncol):
        wide_ref[b * k : (b + 1) * k, b * rdev : (b + 1) * rdev] = r
    left = jnp.concatenate([vecs[b * rows : (b + 1) * rows] for b in range(ncol)], axis=1)
    part = dot3(left, wide_ref[...], NT)
    norm = as_row(jnp.sum(r * r, axis=1, keepdims=True))
    each = part_ref.shape[1] - 1
    for c in range(part_ref.shape[0]):
        part_ref[c, :each, :] = part[c * each : (c + 1) * each]
        part_ref[c, each:, :] = norm


def rows_kernel(res_ref, rows_ref, out_ref):
    rdev = res_ref.shape[2]
    r = res_ref[:, 0, :]
    both = jnp.concatenate([r, exactly(picker(rows_ref, rdev), r, NN, False)], axis=1)
    for c in range(out_ref.shape[0]):
        out_ref[c] = both


def vecs_kernel(vecs_ref, count_ref, rows_ref, out_ref):
    vecs = masked(vecs_ref, count_ref)
    rdev = vecs.shape[1]
    both = jnp.concatenate([vecs, exactly(picker(rows_ref, rdev), vecs, NN, False)], axis=1)
    for c in range(out_ref.shape[0]):
        out_ref[c] = both


def coarse_kernel(inv_ref, out_ref, *, nnar, maxev, ncol, each):
    nrow, ncols = inv_ref.shape
    per = ncols // maxev
    pad = each + 1
    total = nnar * ncol * per * pad
    p = iota((total, ncols), 0)
    a = p % pad
    q = (p // pad) % per
    b = (p // (pad * per)) % ncol
    c = p // (pad * per * ncol)
    want = jnp.where(a < each, q * maxev + b * (maxev // ncol) + c * each + a, -1)
    pick = (want == iota((total, ncols), 1)).astype(F32).astype(BF16)
    moved = exactly(pick, inv_ref[...], NT, True)
    out_ref[...] = jnp.zeros_like(out_ref)
    span = ncol * per * pad
    for d in range(nnar):
        out_ref[d, :, :nrow] = moved[d * span : (d + 1) * span]


def sum_kernel(got_ref, out_ref):
    total = jnp.sum(got_ref[...], axis=0)
    out_ref[...] = jnp.broadcast_to(total[None], out_ref.shape)


def weave(blocks, a_ref, b_ref):
    half = LANES // 2
    for i in range(0, len(blocks), 2):
        one, two = blocks[i], blocks[i + 1]
        low = iota(one.shape, 1) < half
        at = slice(i * half, i * half + LANES)
        a_ref[:, at] = jnp.where(low, one, pltpu.roll(two, half, 1))
        b_ref[:, at] = jnp.where(low, pltpu.roll(one, half, 1), two)


def spread_rows_kernel(got_ref, own_ref, a_ref, b_ref):
    n, _, width = got_ref.shape
    rdev = width - LANES
    for c in range(n):
        own_ref[:, c * rdev : (c + 1) * rdev] = got_ref[c, :, :rdev]
    weave([got_ref[c, :, rdev:] for c in range(n)], a_ref, b_ref)


def margins(a_ref, b_ref):
    sub, nsub = lax.axis_index("sub"), lax.axis_size("sub")
    even = sub % 2 == 0
    a, b = a_ref[...], b_ref[...]
    lefts = jnp.where(sub == 0, 0.0, jnp.where(even, b, a))
    rights = jnp.where(sub == nsub - 1, 0.0, jnp.where(even, a, b))
    return lefts, rights


def margin_product(a_ref, b_ref, mat_ref):
    lefts, rights = margins(a_ref, b_ref)
    half = lefts.shape[1]
    return dot3(lefts, mat_ref[0, :, :half], NT) + dot3(rights, mat_ref[0, :, half:], NT)


def local_kernel(a_ref, b_ref, mat_ref, own_ref, rows_ref, out_ref):
    local = own_ref[...] + margin_product(a_ref, b_ref, mat_ref)
    pick = picker(rows_ref, local.shape[1])
    out_ref[...] = jnp.concatenate([local, exactly(pick, local, NN, False)], axis=1)


def solve_kernel(got_ref, inv_ref, local_ref, out_ref, beta_ref, wide_ref, *, total, maxev):
    nsub, pad, _ = got_ref.shape
    k = local_ref.shape[0]
    width = local_ref.shape[1]
    nnar, span, _ = inv_ref.shape
    ncol = LANES // k
    chunk = span // ncol
    norms = jnp.sum(got_ref[:, pad - 1, :], axis=0, keepdims=True)
    beta = jnp.sqrt(as_col(norms, k) / total + EPS)
    res = got_ref[...].reshape(nsub * pad, LANES)
    for c in range(nnar):
        for b in range(ncol):
            wide_ref[c * chunk : (c + 1) * chunk, b * LANES : (b + 1) * LANES] = inv_ref[
                c, b * chunk : (b + 1) * chunk, :
            ]
    sol = dot3(res.T, wide_ref[...], NN)
    part = sum(sol[b * k : (b + 1) * k, b * LANES : (b + 1) * LANES] for b in range(ncol))
    both = jnp.concatenate([local_ref[...], part], axis=1) / beta
    for c in range(nnar):
        out_ref[c] = both
    beta_ref[...] = jnp.broadcast_to(beta, beta_ref.shape)


def precond_kernel(got_ref, vecs_ref, own_ref, a_ref, b_ref, mine_ref):
    n, k, width = got_ref.shape
    wide = width - LANES
    rdev = wide - LANES
    maxev = vecs_ref.shape[1]
    sol = jnp.sum(got_ref[:, :, wide:], axis=0)[:, :maxev]
    ends = []
    for c in range(n):
        field = got_ref[c, :, :wide] + dot3(sol, vecs_ref[c], NN)
        own_ref[:, c * rdev : (c + 1) * rdev] = field[:, :rdev]
        ends.append(field[:, rdev:])
    weave(ends, a_ref, b_ref)
    nar = lax.axis_index("nar")
    mine_ref[...] = own_ref[:, pl.ds(pl.multiple_of(nar * rdev, rdev), rdev)]


def ratio(a, n):
    return jnp.where(n > 0, a / jnp.where(n > 0, n, 1.0), 0.0)


def image_kernel(a_ref, b_ref, mat_ref, own_ref, res_ref, beta_ref, image_ref, out_ref):
    k = own_ref.shape[0]
    image = own_ref[...] + margin_product(a_ref, b_ref, mat_ref)
    start = res_ref[:, 0, :] / beta_ref[:, :1]
    n = jnp.sum(start * start, axis=1, keepdims=True)
    a = jnp.sum(start * image, axis=1, keepdims=True)
    off = image - ratio(a, n) * start
    s = jnp.sum(off * off, axis=1, keepdims=True)
    image_ref[...] = image
    row = as_row(n) + pltpu.roll(as_row(a), k, 1) + pltpu.roll(as_row(s), 2 * k, 1)
    out_ref[...] = jnp.broadcast_to(row[None], out_ref.shape)


def end_kernel(got_ref, image_ref, res_ref, iter_ref, pre_ref, beta_ref, next_ref, new_ref, hess_ref, *, total):
    k = image_ref.shape[0]
    stats = got_ref[:, 0, :]
    n_i = stats
    a_i = pltpu.roll(stats, LANES - k, 1)
    s_i = pltpu.roll(stats, LANES - 2 * k, 1)
    n = jnp.sum(n_i, axis=0, keepdims=True)
    a = jnp.sum(a_i, axis=0, keepdims=True)
    h = ratio(a, n)
    gap = ratio(a_i, n_i) - h
    square = jnp.sum(s_i + (n_i * gap) * gap, axis=0, keepdims=True)
    beta = beta_ref[:, :1]
    lost = EPS / (beta * beta)
    a_col = as_col(a, k)
    h00 = a_col / total
    square = as_col(square, k) + a_col * as_col(h, k) * (lost * lost)
    h10 = jnp.sqrt(square / total + EPS)
    start = res_ref[:, 0, :] / beta
    next_ref[:, 0, :] = (image_ref[...] - h00 * start) / h10
    factor = beta * h00 / (h00 * h00 + h10 * h10)
    new_ref[:, 0, :] = iter_ref[:, 0, :] + factor * pre_ref[...]
    hess_ref[...] = jnp.concatenate([as_row(beta)[:, :k], as_row(h00)[:, :k], as_row(h10)[:, :k]], axis=0)


def exchange(blocks, axes):
    return lax.all_to_all(blocks, axes, 0, 0)


def beside(first, second, nsub):
    route_a = [(i, i ^ 1) for i in range(nsub)]
    route_b = [(i, (i + 1 if i % 2 else i - 1) % nsub) for i in range(nsub)]
    return lax.ppermute(first, "sub", route_a), lax.ppermute(second, "sub", route_b)


def times(field, matrix):
    return lax.dot_general(field, matrix, NT, precision=HIGH)


def with_margins(kernel, outs, a, b, matrix, *rest):
    rdev, ext = matrix.shape[1:]
    width = 2 * a.shape[1]
    block = (ext - width) // width

    def whole(x):
        zeros = (0,) * x.ndim
        return pl.BlockSpec(x.shape, lambda i: zeros)

    many = isinstance(outs, tuple)
    return pl.pallas_call(
        kernel,
        grid=(1,),
        out_shape=outs,
        in_specs=[whole(a), whole(b), pl.BlockSpec((1, rdev, width), lambda i: (0, 0, block))]
        + [whole(x) for x in rest],
        out_specs=tuple(whole(x) for x in outs) if many else whole(outs),
        compiler_params=pltpu.CompilerParams(vmem_limit_bytes=32 * 2**20),
    )(a, b, matrix, *rest)


def per_device(
    residual, iterate, stiffness, local_inverse, eigvecs, ev_count, coarse_inverse, send_rows
):
    nsub, nnar = lax.axis_size("sub"), lax.axis_size("nar")
    k, _, rdev = residual.shape
    total = nsub * nnar * rdev
    over = send_rows.shape[2]
    maxev = eigvecs.shape[1]
    own = nnar * rdev
    ncol = LANES // k
    each = maxev // ncol // nnar
    pad = each + 1
    span = coarse_inverse.shape[1] // maxev * ncol * pad

    part = local_call(
        begin_kernel, shape(nnar, pad, LANES), [VMEM, VMEM, SMEM], residual, eigvecs, ev_count,
        scratch=[pltpu.VMEM((LANES, ncol * rdev), F32)],
    )
    part = exchange(part, "nar")
    rows = local_call(rows_kernel, shape(nnar, k, rdev + 2 * over), [VMEM, VMEM], residual, send_rows)
    rows = exchange(rows, "nar")
    inverse = local_call(
        functools.partial(coarse_kernel, nnar=nnar, maxev=maxev, ncol=ncol, each=each),
        shape(nnar, span, LANES), [VMEM], coarse_inverse,
    )
    inverse = exchange(inverse, "nar")
    vecs = local_call(
        vecs_kernel, shape(nnar, maxev, rdev + 2 * over), [VMEM, SMEM, VMEM], eigvecs, ev_count, send_rows
    )
    vecs = exchange(vecs, "nar")
    res = local_call(sum_kernel, shape(nsub, pad, LANES), [VMEM], part)
    res = exchange(res, "sub")

    pieces = (shape(k, own), shape(k, nnar * over), shape(k, nnar * over))
    r_own, to_a, to_b = local_call(spread_rows_kernel, pieces, [VMEM], rows)
    got_a, got_b = beside(to_a, to_b, nsub)
    local = times(r_own, local_inverse[0, :, :own])
    local = with_margins(
        local_kernel, shape(k, rdev + 2 * over), got_a, got_b, local_inverse, local, send_rows
    )

    block, beta = local_call(
        functools.partial(solve_kernel, total=total, maxev=maxev),
        (shape(nnar, k, rdev + 2 * over + LANES), shape(k, LANES)),
        [VMEM, VMEM, VMEM], res, inverse, local,
        scratch=[pltpu.VMEM((nsub * pad, ncol * LANES), F32)],
    )
    block = exchange(block, "nar")
    p_own, to_a, to_b, precond = local_call(
        precond_kernel, pieces + (shape(k, rdev),), [VMEM, VMEM], block, vecs
    )

    got_a, got_b = beside(to_a, to_b, nsub)
    image = times(p_own, stiffness[0, :, :own])
    image, stats = with_margins(
        image_kernel, (shape(k, rdev), shape(nsub * nnar, 1, LANES)),
        got_a, got_b, stiffness, image, residual, beta,
    )
    stats = exchange(stats, ("sub", "nar"))
    return local_call(
        functools.partial(end_kernel, total=total),
        (shape(k, 1, rdev), shape(k, 1, rdev), shape(3, k)),
        [VMEM] * 6, stats, image, residual, iterate, precond, beta,
    )


def solution(mesh):
    return jax.shard_map(
        per_device,
        mesh=mesh,
        in_specs=(
            P(None, "sub", "nar"),
            P(None, "sub", "nar"),
            P("sub", "nar", None),
            P("sub", "nar", None),
            P("sub", None, "nar"),
            P("sub"),
            P("sub", "nar"),
            P(None, "sub", "nar"),
        ),
        out_specs=(P(None, "sub", "nar"), P(None, "sub", "nar"), P()),
        check_vma=False,
    )
```

```python
import functools

import jax
import jax.numpy as jnp
from jax import lax
from jax.experimental import pallas as pl
from jax.experimental.pallas import tpu as pltpu
from jax.sharding import PartitionSpec as P

EPS = 1e-06
F32, BF16 = jnp.float32, jnp.bfloat16
LANES = 128
NT = (((1,), (1,)), ((), ()))
NN = (((1,), (0,)), ((), ()))


def shape(*dims):
    return jax.ShapeDtypeStruct(dims, F32)


def whole(x):
    zeros = (0,) * len(x.shape)
    return pl.BlockSpec(x.shape, lambda i: zeros)


def local_call(body, outs, *args, specs=None, scratch=(), limit=4, cost=1):
    many = isinstance(outs, tuple)
    specs = specs or {}
    return pl.pallas_call(
        body,
        grid=(1,),
        out_shape=outs,
        in_specs=[specs.get(i) or whole(x) for i, x in enumerate(args)],
        out_specs=tuple(whole(x) for x in outs) if many else whole(outs),
        scratch_shapes=scratch,
        compiler_params=pltpu.CompilerParams(vmem_limit_bytes=limit * 2**20),
        cost_estimate=pl.CostEstimate(flops=int(cost * 1e9), bytes_accessed=1024, transcendentals=0),
    )(*args)


def halves(x):
    high = x.astype(BF16)
    return high, (x - high.astype(F32)).astype(BF16)


def dot3(a, b, dims):
    dot = functools.partial(lax.dot_general, dimension_numbers=dims, preferred_element_type=F32)
    (ah, al), (bh, bl) = halves(a), halves(b)
    return dot(ah, bh) + (dot(al, bh) + dot(ah, bl))


def exactly(pick, x, dims, first):
    high = x.astype(BF16)
    rest = x - high.astype(F32)
    mid = rest.astype(BF16)
    low = (rest - mid.astype(F32)).astype(BF16)
    total = None
    for part in (low, mid, high):
        pair = (pick, part) if first else (part, pick)
        term = lax.dot_general(*pair, dimension_numbers=dims, preferred_element_type=F32)
        total = term if total is None else total + term
    return total


def iota(dims, axis):
    return lax.broadcasted_iota(jnp.int32, dims, axis)


def as_row(col):
    k = col.shape[0]
    return jnp.sum(jnp.where(iota((k, LANES), 0) == iota((k, LANES), 1), col, 0.0), axis=0, keepdims=True)


def as_col(row, k):
    return jnp.sum(jnp.where(iota((k, LANES), 0) == iota((k, LANES), 1), row, 0.0), axis=1, keepdims=True)


def own_list(rows_ref):
    even = lax.axis_index("sub") % 2 == 0
    rights, lefts = rows_ref[0], rows_ref[1]
    return jnp.concatenate([jnp.where(even, rights, lefts), jnp.where(even, lefts, rights)], axis=1)


def pick_of(listed, rdev):
    return (iota((rdev, LANES), 0).astype(F32) == listed).astype(F32).astype(BF16)


def masked(vecs_ref, count_ref):
    vecs = vecs_ref[0]
    return jnp.where(iota(vecs.shape, 0) < count_ref[0], vecs, 0.0)


def begin_kernel(
    res_hbm, vecs_hbm, inv_hbm, rows_hbm, count_ref, out_ref,
    wide_ref, res_ref, vecs_ref, inv_ref, rows_ref, sems, *, each
):
    pairs = ((res_hbm, res_ref), (vecs_hbm, vecs_ref), (inv_hbm, inv_ref), (rows_hbm, rows_ref))
    copies = [pltpu.make_async_copy(one, two, sems.at[i]) for i, (one, two) in enumerate(pairs)]
    for copy in copies:
        copy.start()
    wide_ref[...] = jnp.zeros_like(wide_ref)
    out_ref[...] = jnp.zeros_like(out_ref)
    for copy in copies:
        copy.wait()
    k, _, rdev = res_ref.shape
    r = res_ref[:, 0, :]
    vecs = masked(vecs_ref, count_ref)
    maxev = vecs.shape[0]
    ncol = LANES // k
    rows = maxev // ncol
    for b in range(ncol):
        wide_ref[b * k : (b + 1) * k, b * rdev : (b + 1) * rdev] = r
    left = jnp.concatenate([vecs[b * rows : (b + 1) * rows] for b in range(ncol)], axis=1)
    part = dot3(left, wide_ref[...], NT)
    norm = as_row(jnp.sum(r * r, axis=1, keepdims=True))
    listed = own_list(rows_ref).astype(F32)
    nnar = out_ref.shape[0]
    moved = coarse_columns(inv_ref[...], nnar=nnar, maxev=maxev, ncol=ncol, each=each)
    span = moved.shape[0] // nnar
    at = rdev // LANES * k
    for c in range(nnar):
        for i in range(rdev // LANES):
            out_ref[c, i * k : (i + 1) * k, :] = r[:, i * LANES : (i + 1) * LANES]
        out_ref[c, at : at + each, :] = part[c * each : (c + 1) * each]
        out_ref[c, at + each : at + each + 1, :] = norm
        out_ref[c, at + each + 1 : at + each + 2, :] = listed
        out_ref[c, at + 8 :, :maxev] = moved[c * span : (c + 1) * span]


def coarse_columns(inverse, *, nnar, maxev, ncol, each):
    ncols = inverse.shape[1]
    per = ncols // maxev
    p = iota((1, ncols), 1)
    a = p % each
    q = (p // each) % per
    b = (p // (each * per)) % ncol
    c = p // (each * per * ncol)
    want = q * maxev + b * (maxev // ncol) + c * each + a
    pick = (want == iota((ncols, ncols), 0)).astype(F32).astype(BF16)
    return exactly(pick, inverse, NN, False).T


def weave(ends, a_ref, b_ref):
    half = LANES // 2
    for i in range(0, len(ends), 2):
        one, two = ends[i], ends[i + 1]
        low = iota(one.shape, 1) < half
        at = slice(i * half, i * half + LANES)
        a_ref[:, at] = jnp.where(low, one, pltpu.roll(two, half, 1))
        b_ref[:, at] = jnp.where(low, pltpu.roll(one, half, 1), two)


def sum_kernel(got_ref, after_ref, out_ref):
    del after_ref
    total = jnp.sum(got_ref[...], axis=0)[: out_ref.shape[1]]
    out_ref[...] = jnp.broadcast_to(total[None], out_ref.shape)


def middle_kernel(got_ref, own_ref, a_ref, b_ref):
    n, _, lanes = got_ref.shape
    k = own_ref.shape[0]
    rdev = own_ref.shape[1] // n
    halves_of = rdev // lanes
    at = halves_of * k
    ends = []
    for c in range(n):
        field = jnp.concatenate([got_ref[c, i * k : (i + 1) * k, :] for i in range(halves_of)], axis=1)
        own_ref[:, c * rdev : (c + 1) * rdev] = field
        listed = got_ref[c, at + 4 : at + 5, :]
        ends.append(exactly(pick_of(listed, rdev), field, NN, False))
    weave(ends, a_ref, b_ref)


def margins(a_ref, b_ref):
    sub, nsub = lax.axis_index("sub"), lax.axis_size("sub")
    even = sub % 2 == 0
    a, b = a_ref[...], b_ref[...]
    lefts = jnp.where(sub == 0, 0.0, jnp.where(even, b, a))
    rights = jnp.where(sub == nsub - 1, 0.0, jnp.where(even, a, b))
    return lefts, rights


def product_kernel(field_ref, mat_ref, out_ref, high_ref, low_ref):
    own = field_ref.shape[1]
    out_ref[...] = dot3(field_ref[...], mat_ref[0, :, :own], NT)
    high_ref[...], low_ref[...] = halves(mat_ref[0, :, own:])


def margin_product(a_ref, b_ref, high_ref, low_ref):
    dot = functools.partial(lax.dot_general, dimension_numbers=NT, preferred_element_type=F32)
    high, low = halves(jnp.concatenate(margins(a_ref, b_ref), axis=1))
    return dot(high, high_ref[...]) + (dot(low, high_ref[...]) + dot(high, low_ref[...]))


def local_kernel(a_ref, b_ref, own_ref, high_ref, low_ref, *refs):
    vecs, (out_ref, vecs_ref) = refs[:-2], refs[-2:]
    out_ref[...] = own_ref[...] + margin_product(a_ref, b_ref, high_ref, low_ref)
    for i, ref in enumerate(vecs):
        vecs_ref[i] = ref[0]


def solve_kernel(got_ref, one_ref, two_ref, local_ref, out_ref, beta_ref, wide_ref, *, total, maxev):
    nsub, pad, _ = got_ref.shape
    k = local_ref.shape[0]
    each = pad - 1
    nnar = one_ref.shape[0]
    ncol = LANES // k
    per = nsub // nnar
    chunk = per * each
    norms = jnp.sum(got_ref[:, pad - 1, :], axis=0, keepdims=True)
    beta = jnp.sqrt(as_col(norms, k) / total + EPS)
    res = got_ref[...].reshape(nsub * pad, LANES)
    wide_ref[...] = jnp.zeros_like(wide_ref)
    for c in range(nnar):
        for b in range(ncol):
            ref, at = (one_ref, b * chunk) if b < ncol // 2 else (two_ref, (b - ncol // 2) * chunk)
            piece = ref[c, at : at + chunk, :]
            for q in range(per):
                to = (c * per + q) * pad
                wide_ref[to : to + each, b * LANES : (b + 1) * LANES] = piece[q * each : (q + 1) * each]
    sol = dot3(res.T, wide_ref[...], NN)
    part = sum(sol[b * k : (b + 1) * k, b * LANES : (b + 1) * LANES] for b in range(ncol))
    both = jnp.concatenate([local_ref[...], part], axis=1) / beta
    for c in range(nnar):
        out_ref[c] = both
    beta_ref[...] = jnp.broadcast_to(beta, beta_ref.shape)


def precond_kernel(got_ref, lists_ref, count_ref, even_ref, odd_ref, own_ref, a_ref, b_ref, mine_ref):
    n, k, width = got_ref.shape
    rdev = width - LANES
    maxev = even_ref.shape[1]
    nar = lax.axis_index("nar")
    sol = jnp.sum(got_ref[:, :, rdev:], axis=0)
    sol = jnp.where(iota(sol.shape, 1) < count_ref[0], sol, 0.0)[:, :maxev]
    for i in range(n):
        field = got_ref[nar ^ i, :, :rdev] + dot3(sol, (odd_ref if i % 2 else even_ref)[i // 2], NN)
        own_ref[:, pl.ds(pl.multiple_of((nar ^ i) * rdev, rdev), rdev)] = field
        if i == 0:
            mine_ref[...] = field
    ends = [
        exactly(pick_of(lists_ref[c, 4:5, :], rdev), own_ref[:, c * rdev : (c + 1) * rdev], NN, False)
        for c in range(n)
    ]
    weave(ends, a_ref, b_ref)


def ratio(a, n):
    return jnp.where(n > 0, a / jnp.where(n > 0, n, 1.0), 0.0)


def image_kernel(a_ref, b_ref, own_ref, high_ref, low_ref, res_ref, beta_ref, image_ref, out_ref):
    k = own_ref.shape[0]
    image = own_ref[...] + margin_product(a_ref, b_ref, high_ref, low_ref)
    start = res_ref[:, 0, :] / beta_ref[:, :1]
    n = jnp.sum(start * start, axis=1, keepdims=True)
    a = jnp.sum(start * image, axis=1, keepdims=True)
    off = image - ratio(a, n) * start
    s = jnp.sum(off * off, axis=1, keepdims=True)
    image_ref[...] = image
    row = as_row(n) + pltpu.roll(as_row(a), k, 1) + pltpu.roll(as_row(s), 2 * k, 1)
    out_ref[...] = jnp.broadcast_to(row[None], out_ref.shape)


def end_kernel(got_ref, image_ref, res_ref, iter_ref, pre_ref, beta_ref, next_ref, new_ref, hess_ref, *, total):
    k = image_ref.shape[0]
    stats = got_ref[:, 0, :]
    n_i = stats
    a_i = pltpu.roll(stats, LANES - k, 1)
    s_i = pltpu.roll(stats, LANES - 2 * k, 1)
    n = jnp.sum(n_i, axis=0, keepdims=True)
    a = jnp.sum(a_i, axis=0, keepdims=True)
    h = ratio(a, n)
    gap = ratio(a_i, n_i) - h
    square = jnp.sum(s_i + (n_i * gap) * gap, axis=0, keepdims=True)
    beta = beta_ref[:, :1]
    lost = EPS / (beta * beta)
    a_col = as_col(a, k)
    h00 = a_col / total
    square = as_col(square, k) + a_col * as_col(h, k) * (lost * lost)
    h10 = jnp.sqrt(square / total + EPS)
    start = res_ref[:, 0, :] / beta
    next_ref[:, 0, :] = (image_ref[...] - h00 * start) / h10
    factor = beta * h00 / (h00 * h00 + h10 * h10)
    new_ref[:, 0, :] = iter_ref[:, 0, :] + factor * pre_ref[...]
    hess_ref[...] = jnp.concatenate([as_row(beta)[:, :k], as_row(h00)[:, :k], as_row(h10)[:, :k]], axis=0)


def exchange(blocks, axes):
    return lax.all_to_all(blocks, axes, 0, 0)


def beside(first, second, nsub):
    route_a = [(i, i ^ 1) for i in range(nsub)]
    route_b = [(i, (i + 1 if i % 2 else i - 1) % nsub) for i in range(nsub)]
    return lax.ppermute(first, "sub", route_a), lax.ppermute(second, "sub", route_b)


def across(block, n, mask):
    return lax.ppermute(block, "nar", [(i, i ^ mask) for i in range(n)])


def product(field, matrix):
    rdev, ext = matrix.shape[1:]
    split = jax.ShapeDtypeStruct((rdev, ext - field.shape[1]), BF16)
    return local_call(product_kernel, (shape(field.shape[0], rdev), split, split), field, matrix, limit=10)


def per_device(
    residual, iterate, stiffness, local_inverse, eigvecs, ev_count, coarse_inverse, send_rows
):
    nsub, nnar = lax.axis_size("sub"), lax.axis_size("nar")
    k, _, rdev = residual.shape
    total = nsub * nnar * rdev
    over = send_rows.shape[2]
    maxev = eigvecs.shape[1]
    own = nnar * rdev
    ncol = LANES // k
    each = maxev // ncol // nnar
    pad = each + 1
    span = coarse_inverse.shape[1] // nnar
    head = rdev // LANES * k
    smem = pl.BlockSpec(memory_space=pltpu.SMEM)
    hbm = pl.BlockSpec(memory_space=pltpu.HBM)

    vecs = [eigvecs] + [across(eigvecs, nnar, m) for m in range(2, nnar, 2)]

    part = local_call(
        functools.partial(begin_kernel, each=each),
        shape(nnar, head + 8 + span, LANES), residual, eigvecs, coarse_inverse, send_rows, ev_count,
        specs={0: hbm, 1: hbm, 2: hbm, 3: hbm, 4: smem},
        scratch=[
            pltpu.VMEM((LANES, ncol * rdev), F32),
            pltpu.VMEM(residual.shape, F32),
            pltpu.VMEM(eigvecs.shape, F32),
            pltpu.VMEM(coarse_inverse.shape, F32),
            pltpu.VMEM(send_rows.shape, jnp.int32),
            pltpu.SemaphoreType.DMA((4,)),
        ],
        limit=60,
    )
    part = exchange(part, "nar")
    lists = pl.BlockSpec((nnar, 8, LANES), lambda i: (0, head // 8, 0))
    pieces = (shape(k, own), shape(k, nnar * over), shape(k, nnar * over))
    r_own, to_a, to_b = local_call(
        middle_kernel, pieces, part,
        specs={0: pl.BlockSpec((nnar, head + 8, LANES), lambda i: (0, 0, 0))},
    )
    res = local_call(
        sum_kernel, shape(nsub, pad, LANES), part, to_b, specs={0: lists, 1: hbm}, cost=10
    )
    res = exchange(res, "sub")

    got_a, got_b = beside(to_a, to_b, nsub)
    local, vecs = local_call(
        local_kernel, (shape(k, rdev), shape(nnar // 2, maxev, rdev)),
        got_a, got_b, *product(r_own, local_inverse), *vecs,
    )
    vecs = (vecs, across(vecs, nnar, 1))

    first = (head + 8) // (span // 2)
    block, beta = local_call(
        functools.partial(solve_kernel, total=total, maxev=maxev),
        (shape(nnar, k, rdev + LANES), shape(k, LANES)), res, part, part, local,
        specs={
            j + 1: pl.BlockSpec((nnar, span // 2, LANES), lambda i, j=j: (0, first + j, 0))
            for j in range(2)
        },
        scratch=[pltpu.VMEM((nsub * pad, ncol * LANES), F32)],
    )
    block = exchange(block, "nar")
    p_own, to_a, to_b, precond = local_call(
        precond_kernel, pieces + (shape(k, rdev),), block, part, ev_count, *vecs,
        specs={1: lists, 2: smem},
    )

    got_a, got_b = beside(to_a, to_b, nsub)
    image, stats = local_call(
        image_kernel, (shape(k, rdev), shape(nsub * nnar, 1, LANES)),
        got_a, got_b, *product(p_own, stiffness), residual, beta,
    )
    stats = exchange(stats, ("sub", "nar"))
    return local_call(
        functools.partial(end_kernel, total=total),
        (shape(k, 1, rdev), shape(k, 1, rdev), shape(3, k)),
        stats, image, residual, iterate, precond, beta,
    )


def solution(mesh):
    return jax.shard_map(
        per_device,
        mesh=mesh,
        in_specs=(
            P(None, "sub", "nar"),
            P(None, "sub", "nar"),
            P("sub", "nar", None),
            P("sub", "nar", None),
            P("sub", None, "nar"),
            P("sub"),
            P("sub", "nar"),
            P(None, "sub", "nar"),
        ),
        out_specs=(P(None, "sub", "nar"), P(None, "sub", "nar"), P()),
        check_vma=False,
    )
```

```python
import functools

import jax
import jax.numpy as jnp
from jax import lax
from jax.experimental import pallas as pl
from jax.experimental.pallas import tpu as pltpu
from jax.sharding import PartitionSpec as P

EPS = 1e-06
F32, BF16 = jnp.float32, jnp.bfloat16
LANES = 128
NT = (((1,), (1,)), ((), ()))
NN = (((1,), (0,)), ((), ()))


def shape(*dims):
    return jax.ShapeDtypeStruct(dims, F32)


def whole(x):
    zeros = (0,) * len(x.shape)
    return pl.BlockSpec(x.shape, lambda i: zeros)


def local_call(body, outs, *args, specs=None, scratch=(), limit=4, cost=1):
    many = isinstance(outs, tuple)
    specs = specs or {}
    return pl.pallas_call(
        body,
        grid=(1,),
        out_shape=outs,
        in_specs=[specs.get(i) or whole(x) for i, x in enumerate(args)],
        out_specs=tuple(whole(x) for x in outs) if many else whole(outs),
        scratch_shapes=scratch,
        compiler_params=pltpu.CompilerParams(vmem_limit_bytes=limit * 2**20),
        cost_estimate=pl.CostEstimate(flops=int(cost * 1e9), bytes_accessed=1024, transcendentals=0),
    )(*args)


def halves(x):
    high = x.astype(BF16)
    return high, (x - high.astype(F32)).astype(BF16)


def dot3(a, b, dims):
    dot = functools.partial(lax.dot_general, dimension_numbers=dims, preferred_element_type=F32)
    (ah, al), (bh, bl) = halves(a), halves(b)
    return dot(ah, bh) + (dot(al, bh) + dot(ah, bl))


def exactly(pick, x, dims, first):
    high = x.astype(BF16)
    rest = x - high.astype(F32)
    mid = rest.astype(BF16)
    low = (rest - mid.astype(F32)).astype(BF16)
    total = None
    for part in (low, mid, high):
        pair = (pick, part) if first else (part, pick)
        term = lax.dot_general(*pair, dimension_numbers=dims, preferred_element_type=F32)
        total = term if total is None else total + term
    return total


def iota(dims, axis):
    return lax.broadcasted_iota(jnp.int32, dims, axis)


def as_row(col):
    k = col.shape[0]
    return jnp.sum(jnp.where(iota((k, LANES), 0) == iota((k, LANES), 1), col, 0.0), axis=0, keepdims=True)


def as_col(row, k):
    return jnp.sum(jnp.where(iota((k, LANES), 0) == iota((k, LANES), 1), row, 0.0), axis=1, keepdims=True)


def own_list(rows_ref):
    even = lax.axis_index("sub") % 2 == 0
    rights, lefts = rows_ref[0], rows_ref[1]
    return jnp.concatenate([jnp.where(even, rights, lefts), jnp.where(even, lefts, rights)], axis=1)


def pick_of(listed, rdev):
    return (iota((rdev, LANES), 0).astype(F32) == listed).astype(F32).astype(BF16)


def masked(vecs_ref, count_ref):
    vecs = vecs_ref[0]
    return jnp.where(iota(vecs.shape, 0) < count_ref[0], vecs, 0.0)


def begin_kernel(
    res_hbm, vecs_hbm, inv_hbm, rows_hbm, count_ref, out_ref,
    wide_ref, res_ref, vecs_ref, inv_ref, rows_ref, sems, *, each
):
    pairs = ((res_hbm, res_ref), (vecs_hbm, vecs_ref), (inv_hbm, inv_ref), (rows_hbm, rows_ref))
    copies = [pltpu.make_async_copy(one, two, sems.at[i]) for i, (one, two) in enumerate(pairs)]
    for copy in copies:
        copy.start()
    wide_ref[...] = jnp.zeros_like(wide_ref)
    out_ref[...] = jnp.zeros_like(out_ref)
    for copy in copies:
        copy.wait()
    k, _, rdev = res_ref.shape
    r = res_ref[:, 0, :]
    vecs = masked(vecs_ref, count_ref)
    maxev = vecs.shape[0]
    ncol = LANES // k
    rows = maxev // ncol
    for b in range(ncol):
        wide_ref[b * k : (b + 1) * k, b * rdev : (b + 1) * rdev] = r
    left = jnp.concatenate([vecs[b * rows : (b + 1) * rows] for b in range(ncol)], axis=1)
    part = dot3(left, wide_ref[...], NT)
    norm = as_row(jnp.sum(r * r, axis=1, keepdims=True))
    listed = own_list(rows_ref).astype(F32)
    nnar = out_ref.shape[0]
    moved = coarse_columns(inv_ref[...], nnar=nnar, maxev=maxev, ncol=ncol, each=each)
    span = moved.shape[0] // nnar
    at = rdev // LANES * k
    for c in range(nnar):
        for i in range(rdev // LANES):
            out_ref[c, i * k : (i + 1) * k, :] = r[:, i * LANES : (i + 1) * LANES]
        out_ref[c, at : at + each, :] = part[c * each : (c + 1) * each]
        out_ref[c, at + each : at + each + 1, :] = norm
        out_ref[c, at + each + 1 : at + each + 2, :] = listed
        out_ref[c, at + 8 :, :maxev] = moved[c * span : (c + 1) * span]


def coarse_columns(inverse, *, nnar, maxev, ncol, each):
    ncols = inverse.shape[1]
    per = ncols // maxev
    p = iota((1, ncols), 1)
    a = p % each
    q = (p // each) % per
    b = (p // (each * per)) % ncol
    c = p // (each * per * ncol)
    want = q * maxev + b * (maxev // ncol) + c * each + a
    pick = (want == iota((ncols, ncols), 0)).astype(F32).astype(BF16)
    return exactly(pick, inverse, NN, False).T


def weave(ends, out_ref):
    half = LANES // 2
    core = lax.axis_index("nar") % 2
    low = iota(ends[0].shape, 1) < half
    for i in range(0, len(ends), 2):
        one, two = ends[i], ends[i + 1]
        first = jnp.where(low, one, pltpu.roll(two, half, 1))
        second = jnp.where(low, pltpu.roll(one, half, 1), two)
        out_ref[:, i * half : i * half + LANES] = jnp.where(core == 0, first, second)


def sum_kernel(got_ref, after_ref, out_ref):
    del after_ref
    total = jnp.sum(got_ref[...], axis=0)[: out_ref.shape[1]]
    out_ref[...] = jnp.broadcast_to(total[None], out_ref.shape)


def middle_kernel(got_ref, own_ref, send_ref):
    n, _, lanes = got_ref.shape
    k = own_ref.shape[0]
    rdev = own_ref.shape[1] // n
    halves_of = rdev // lanes
    at = halves_of * k
    ends = []
    for c in range(n):
        field = jnp.concatenate([got_ref[c, i * k : (i + 1) * k, :] for i in range(halves_of)], axis=1)
        own_ref[:, c * rdev : (c + 1) * rdev] = field
        listed = got_ref[c, at + 4 : at + 5, :]
        ends.append(exactly(pick_of(listed, rdev), field, NN, False))
    weave(ends, send_ref)


def margins(got_ref, other_ref):
    sub, nsub = lax.axis_index("sub"), lax.axis_size("sub")
    core = lax.axis_index("nar") % 2
    right = sub % 2 == core
    got, other = got_ref[...], other_ref[...]
    lefts = jnp.where(sub == 0, 0.0, jnp.where(right, other, got))
    rights = jnp.where(sub == nsub - 1, 0.0, jnp.where(right, got, other))
    return lefts, rights


def product_kernel(field_ref, mat_ref, out_ref, high_ref, low_ref):
    own = field_ref.shape[1]
    out_ref[...] = dot3(field_ref[...], mat_ref[0, :, :own], NT)
    high_ref[...], low_ref[...] = halves(mat_ref[0, :, own:])


def margin_product(a_ref, b_ref, high_ref, low_ref):
    dot = functools.partial(lax.dot_general, dimension_numbers=NT, preferred_element_type=F32)
    high, low = halves(jnp.concatenate(margins(a_ref, b_ref), axis=1))
    return dot(high, high_ref[...]) + (dot(low, high_ref[...]) + dot(high, low_ref[...]))


def local_kernel(a_ref, b_ref, own_ref, high_ref, low_ref, *refs):
    vecs, (out_ref, vecs_ref) = refs[:-2], refs[-2:]
    out_ref[...] = own_ref[...] + margin_product(a_ref, b_ref, high_ref, low_ref)
    for i, ref in enumerate(vecs):
        vecs_ref[i] = ref[0]


def solve_kernel(got_ref, one_ref, two_ref, local_ref, out_ref, beta_ref, wide_ref, *, total, maxev):
    nsub, pad, _ = got_ref.shape
    k = local_ref.shape[0]
    each = pad - 1
    nnar = one_ref.shape[0]
    ncol = LANES // k
    per = nsub // nnar
    chunk = per * each
    norms = jnp.sum(got_ref[:, pad - 1, :], axis=0, keepdims=True)
    beta = jnp.sqrt(as_col(norms, k) / total + EPS)
    res = got_ref[...].reshape(nsub * pad, LANES)
    wide_ref[...] = jnp.zeros_like(wide_ref)
    for c in range(nnar):
        for b in range(ncol):
            ref, at = (one_ref, b * chunk) if b < ncol // 2 else (two_ref, (b - ncol // 2) * chunk)
            piece = ref[c, at : at + chunk, :]
            for q in range(per):
                to = (c * per + q) * pad
                wide_ref[to : to + each, b * LANES : (b + 1) * LANES] = piece[q * each : (q + 1) * each]
    sol = dot3(res.T, wide_ref[...], NN)
    part = sum(sol[b * k : (b + 1) * k, b * LANES : (b + 1) * LANES] for b in range(ncol))
    both = jnp.concatenate([local_ref[...], part], axis=1) / beta
    for c in range(nnar):
        out_ref[c] = both
    beta_ref[...] = jnp.broadcast_to(beta, beta_ref.shape)


def precond_kernel(got_ref, lists_ref, count_ref, even_ref, odd_ref, own_ref, send_ref, mine_ref):
    n, k, width = got_ref.shape
    rdev = width - LANES
    maxev = even_ref.shape[1]
    nar = lax.axis_index("nar")
    sol = jnp.sum(got_ref[:, :, rdev:], axis=0)
    sol = jnp.where(iota(sol.shape, 1) < count_ref[0], sol, 0.0)[:, :maxev]
    for i in range(n):
        field = got_ref[nar ^ i, :, :rdev] + dot3(sol, (odd_ref if i % 2 else even_ref)[i // 2], NN)
        own_ref[:, pl.ds(pl.multiple_of((nar ^ i) * rdev, rdev), rdev)] = field
        if i == 0:
            mine_ref[...] = field
    ends = [
        exactly(pick_of(lists_ref[c, 4:5, :], rdev), own_ref[:, c * rdev : (c + 1) * rdev], NN, False)
        for c in range(n)
    ]
    weave(ends, send_ref)


def ratio(a, n):
    return jnp.where(n > 0, a / jnp.where(n > 0, n, 1.0), 0.0)


def image_kernel(a_ref, b_ref, own_ref, high_ref, low_ref, res_ref, beta_ref, image_ref, out_ref):
    k = own_ref.shape[0]
    image = own_ref[...] + margin_product(a_ref, b_ref, high_ref, low_ref)
    start = res_ref[:, 0, :] / beta_ref[:, :1]
    n = jnp.sum(start * start, axis=1, keepdims=True)
    a = jnp.sum(start * image, axis=1, keepdims=True)
    off = image - ratio(a, n) * start
    s = jnp.sum(off * off, axis=1, keepdims=True)
    image_ref[...] = image
    row = as_row(n) + pltpu.roll(as_row(a), k, 1) + pltpu.roll(as_row(s), 2 * k, 1)
    out_ref[...] = jnp.broadcast_to(row[None], out_ref.shape)


def end_kernel(got_ref, image_ref, res_ref, iter_ref, pre_ref, beta_ref, next_ref, new_ref, hess_ref, *, total):
    k = image_ref.shape[0]
    stats = got_ref[:, 0, :]
    n_i = stats
    a_i = pltpu.roll(stats, LANES - k, 1)
    s_i = pltpu.roll(stats, LANES - 2 * k, 1)
    n = jnp.sum(n_i, axis=0, keepdims=True)
    a = jnp.sum(a_i, axis=0, keepdims=True)
    h = ratio(a, n)
    gap = ratio(a_i, n_i) - h
    square = jnp.sum(s_i + (n_i * gap) * gap, axis=0, keepdims=True)
    beta = beta_ref[:, :1]
    lost = EPS / (beta * beta)
    a_col = as_col(a, k)
    h00 = a_col / total
    square = as_col(square, k) + a_col * as_col(h, k) * (lost * lost)
    h10 = jnp.sqrt(square / total + EPS)
    start = res_ref[:, 0, :] / beta
    next_ref[:, 0, :] = (image_ref[...] - h00 * start) / h10
    factor = beta * h00 / (h00 * h00 + h10 * h10)
    new_ref[:, 0, :] = iter_ref[:, 0, :] + factor * pre_ref[...]
    hess_ref[...] = jnp.concatenate([as_row(beta)[:, :k], as_row(h00)[:, :k], as_row(h10)[:, :k]], axis=0)


def exchange(blocks, axes):
    return lax.all_to_all(blocks, axes, 0, 0)


def beside(block, nsub, nnar):
    def partner(sub, nar):
        if nar % 2 == 0:
            return sub ^ 1
        return (sub + 1 if sub % 2 else sub - 1) % nsub

    route = [
        (sub * nnar + nar, partner(sub, nar) * nnar + nar) for sub in range(nsub) for nar in range(nnar)
    ]
    got = lax.ppermute(block, ("sub", "nar"), route)
    return got, across(got, nnar, 1)


def across(block, n, mask):
    return lax.ppermute(block, "nar", [(i, i ^ mask) for i in range(n)])


def product(field, matrix):
    rdev, ext = matrix.shape[1:]
    split = jax.ShapeDtypeStruct((rdev, ext - field.shape[1]), BF16)
    return local_call(product_kernel, (shape(field.shape[0], rdev), split, split), field, matrix, limit=10)


def per_device(
    residual, iterate, stiffness, local_inverse, eigvecs, ev_count, coarse_inverse, send_rows
):
    nsub, nnar = lax.axis_size("sub"), lax.axis_size("nar")
    k, _, rdev = residual.shape
    total = nsub * nnar * rdev
    over = send_rows.shape[2]
    maxev = eigvecs.shape[1]
    own = nnar * rdev
    ncol = LANES // k
    each = maxev // ncol // nnar
    pad = each + 1
    span = coarse_inverse.shape[1] // nnar
    head = rdev // LANES * k
    smem = pl.BlockSpec(memory_space=pltpu.SMEM)
    hbm = pl.BlockSpec(memory_space=pltpu.HBM)

    vecs = [eigvecs] + [across(eigvecs, nnar, m) for m in range(2, nnar, 2)]

    part = local_call(
        functools.partial(begin_kernel, each=each),
        shape(nnar, head + 8 + span, LANES), residual, eigvecs, coarse_inverse, send_rows, ev_count,
        specs={0: hbm, 1: hbm, 2: hbm, 3: hbm, 4: smem},
        scratch=[
            pltpu.VMEM((LANES, ncol * rdev), F32),
            pltpu.VMEM(residual.shape, F32),
            pltpu.VMEM(eigvecs.shape, F32),
            pltpu.VMEM(coarse_inverse.shape, F32),
            pltpu.VMEM(send_rows.shape, jnp.int32),
            pltpu.SemaphoreType.DMA((4,)),
        ],
        limit=60,
    )
    part = exchange(part, "nar")
    lists = pl.BlockSpec((nnar, 8, LANES), lambda i: (0, head // 8, 0))
    pieces = (shape(k, own), shape(k, nnar * over))
    r_own, send = local_call(
        middle_kernel, pieces, part,
        specs={0: pl.BlockSpec((nnar, head + 8, LANES), lambda i: (0, 0, 0))},
    )
    res = local_call(
        sum_kernel, shape(nsub, pad, LANES), part, send, specs={0: lists, 1: hbm}, cost=10
    )
    res = exchange(res, "sub")

    got = beside(send, nsub, nnar)
    local, vecs = local_call(
        local_kernel, (shape(k, rdev), shape(nnar // 2, maxev, rdev)),
        *got, *product(r_own, local_inverse), *vecs,
    )
    vecs = (vecs, across(vecs, nnar, 1))

    first = (head + 8) // (span // 2)
    block, beta = local_call(
        functools.partial(solve_kernel, total=total, maxev=maxev),
        (shape(nnar, k, rdev + LANES), shape(k, LANES)), res, part, part, local,
        specs={
            j + 1: pl.BlockSpec((nnar, span // 2, LANES), lambda i, j=j: (0, first + j, 0))
            for j in range(2)
        },
        scratch=[pltpu.VMEM((nsub * pad, ncol * LANES), F32)],
    )
    block = exchange(block, "nar")
    p_own, send, precond = local_call(
        precond_kernel, pieces + (shape(k, rdev),), block, part, ev_count, *vecs,
        specs={1: lists, 2: smem},
    )

    got = beside(send, nsub, nnar)
    image, stats = local_call(
        image_kernel, (shape(k, rdev), shape(nsub * nnar, 1, LANES)),
        *got, *product(p_own, stiffness), residual, beta,
    )
    stats = exchange(stats, ("sub", "nar"))
    return local_call(
        functools.partial(end_kernel, total=total),
        (shape(k, 1, rdev), shape(k, 1, rdev), shape(3, k)),
        stats, image, residual, iterate, precond, beta,
    )


def solution(mesh):
    return jax.shard_map(
        per_device,
        mesh=mesh,
        in_specs=(
            P(None, "sub", "nar"),
            P(None, "sub", "nar"),
            P("sub", "nar", None),
            P("sub", "nar", None),
            P("sub", None, "nar"),
            P("sub"),
            P("sub", "nar"),
            P(None, "sub", "nar"),
        ),
        out_specs=(P(None, "sub", "nar"), P(None, "sub", "nar"), P()),
        check_vma=False,
    )
```

```python
import functools

import jax
import jax.numpy as jnp
from jax import lax
from jax.experimental import pallas as pl
from jax.experimental.pallas import tpu as pltpu
from jax.sharding import PartitionSpec as P

EPS = 1e-06
COSTS = {'middle_kernel': 0.01, 'product_kernel': 3, 'half_kernel': 1, 'rest_kernel': 1, 'local_kernel': 0.3, 'solve_kernel': 3, 'begin_kernel': 0.3}
F32, BF16 = jnp.float32, jnp.bfloat16
LANES = 128
NT = (((1,), (1,)), ((), ()))
NN = (((1,), (0,)), ((), ()))


def shape(*dims):
    return jax.ShapeDtypeStruct(dims, F32)


def whole(x):
    zeros = (0,) * len(x.shape)
    return pl.BlockSpec(x.shape, lambda i: zeros)


def local_call(body, outs, *args, specs=None, scratch=(), limit=6, cost=1):
    body_name = getattr(body, "func", body).__name__
    cost = COSTS.get(body_name, cost)
    many = isinstance(outs, tuple)
    specs = specs or {}
    return pl.pallas_call(
        body,
        grid=(1,),
        out_shape=outs,
        in_specs=[specs.get(i) or whole(x) for i, x in enumerate(args)],
        out_specs=tuple(whole(x) for x in outs) if many else whole(outs),
        scratch_shapes=scratch,
        compiler_params=pltpu.CompilerParams(vmem_limit_bytes=limit * 2**20),
        cost_estimate=pl.CostEstimate(flops=int(cost * 1e9), bytes_accessed=1024, transcendentals=0),
    )(*args)


def halves(x):
    high = x.astype(BF16)
    return high, (x - high.astype(F32)).astype(BF16)


def dot3(a, b, dims):
    dot = functools.partial(lax.dot_general, dimension_numbers=dims, preferred_element_type=F32)
    (ah, al), (bh, bl) = halves(a), halves(b)
    return dot(ah, bh) + (dot(al, bh) + dot(ah, bl))


def exactly(pick, x, dims, first):
    high = x.astype(BF16)
    rest = x - high.astype(F32)
    mid = rest.astype(BF16)
    low = (rest - mid.astype(F32)).astype(BF16)
    total = None
    for part in (low, mid, high):
        pair = (pick, part) if first else (part, pick)
        term = lax.dot_general(*pair, dimension_numbers=dims, preferred_element_type=F32)
        total = term if total is None else total + term
    return total


def iota(dims, axis):
    return lax.broadcasted_iota(jnp.int32, dims, axis)


def as_row(col):
    k = col.shape[0]
    return jnp.sum(jnp.where(iota((k, LANES), 0) == iota((k, LANES), 1), col, 0.0), axis=0, keepdims=True)


def as_col(row, k):
    return jnp.sum(jnp.where(iota((k, LANES), 0) == iota((k, LANES), 1), row, 0.0), axis=1, keepdims=True)


def own_list(rows_ref):
    even = lax.axis_index("sub") % 2 == 0
    rights, lefts = rows_ref[0], rows_ref[1]
    return jnp.concatenate([jnp.where(even, rights, lefts), jnp.where(even, lefts, rights)], axis=1)


def pick_of(listed, rdev):
    return (iota((rdev, LANES), 0).astype(F32) == listed).astype(F32).astype(BF16)


def masked(vecs_ref, count_ref):
    vecs = vecs_ref[0]
    return jnp.where(iota(vecs.shape, 0) < count_ref[0], vecs, 0.0)


def begin_kernel(
    res_hbm, vecs_hbm, inv_hbm, rows_hbm, count_ref, out_ref,
    wide_ref, res_ref, vecs_ref, inv_ref, rows_ref, sems, *, each
):
    pairs = ((res_hbm, res_ref), (vecs_hbm, vecs_ref), (inv_hbm, inv_ref), (rows_hbm, rows_ref))
    copies = [pltpu.make_async_copy(one, two, sems.at[i]) for i, (one, two) in enumerate(pairs)]
    for copy in copies:
        copy.start()
    wide_ref[...] = jnp.zeros_like(wide_ref)
    out_ref[...] = jnp.zeros_like(out_ref)
    for copy in copies:
        copy.wait()
    k, _, rdev = res_ref.shape
    r = res_ref[:, 0, :]
    vecs = masked(vecs_ref, count_ref)
    maxev = vecs.shape[0]
    ncol = LANES // k
    rows = maxev // ncol
    for b in range(ncol):
        wide_ref[b * k : (b + 1) * k, b * rdev : (b + 1) * rdev] = r
    left = jnp.concatenate([vecs[b * rows : (b + 1) * rows] for b in range(ncol)], axis=1)
    part = dot3(left, wide_ref[...], NT)
    norm = as_row(jnp.sum(r * r, axis=1, keepdims=True))
    listed = own_list(rows_ref).astype(F32)
    nnar = out_ref.shape[0]
    moved = coarse_columns(inv_ref[...], nnar=nnar, maxev=maxev, ncol=ncol, each=each)
    span = moved.shape[0] // nnar
    at = rdev // LANES * k
    for c in range(nnar):
        for i in range(rdev // LANES):
            out_ref[c, i * k : (i + 1) * k, :] = r[:, i * LANES : (i + 1) * LANES]
        out_ref[c, at : at + each, :] = part[c * each : (c + 1) * each]
        out_ref[c, at + each : at + each + 1, :] = norm
        out_ref[c, at + each + 1 : at + each + 2, :] = listed
        out_ref[c, at + 8 :, :maxev] = moved[c * span : (c + 1) * span]


def coarse_columns(inverse, *, nnar, maxev, ncol, each):
    ncols = inverse.shape[1]
    per = ncols // maxev
    p = iota((1, ncols), 1)
    a = p % each
    q = (p // each) % per
    b = (p // (each * per)) % ncol
    c = p // (each * per * ncol)
    want = q * maxev + b * (maxev // ncol) + c * each + a
    pick = (want == iota((ncols, ncols), 0)).astype(F32).astype(BF16)
    return exactly(pick, inverse, NN, False).T


def weave(ends, out_ref):
    half = LANES // 2
    core = lax.axis_index("nar") % 2
    low = iota(ends[0].shape, 1) < half
    for i in range(0, len(ends), 2):
        one, two = ends[i], ends[i + 1]
        first = jnp.where(low, one, pltpu.roll(two, half, 1))
        second = jnp.where(low, pltpu.roll(one, half, 1), two)
        out_ref[:, i * half : i * half + LANES] = jnp.where(core == 0, first, second)


def middle_kernel(got_ref, res_ref, own_ref, send_ref):
    n, _, lanes = got_ref.shape
    pad = res_ref.shape[1]
    k = own_ref.shape[0]
    rdev = own_ref.shape[1] // n
    halves_of = rdev // lanes
    at = halves_of * k
    total = jnp.sum(got_ref[:, at : at + 8, :], axis=0)[:pad]
    res_ref[...] = jnp.broadcast_to(total[None], res_ref.shape)
    ends = []
    for c in range(n):
        field = jnp.concatenate([got_ref[c, i * k : (i + 1) * k, :] for i in range(halves_of)], axis=1)
        own_ref[:, c * rdev : (c + 1) * rdev] = field
        listed = got_ref[c, at + 4 : at + 5, :]
        ends.append(exactly(pick_of(listed, rdev), field, NN, False))
    weave(ends, send_ref)


def margins(got_ref, other_ref):
    sub, nsub = lax.axis_index("sub"), lax.axis_size("sub")
    core = lax.axis_index("nar") % 2
    right = sub % 2 == core
    got, other = got_ref[...], other_ref[...]
    lefts = jnp.where(sub == 0, 0.0, jnp.where(right, other, got))
    rights = jnp.where(sub == nsub - 1, 0.0, jnp.where(right, got, other))
    return lefts, rights


def product_kernel(field_ref, mat_ref, out_ref, high_ref, low_ref):
    own = field_ref.shape[1]
    out_ref[...] = dot3(field_ref[...], mat_ref[0, :, :own], NT)
    high_ref[...], low_ref[...] = halves(mat_ref[0, :, own:])


def half_kernel(field_ref, mat_ref, out_ref):
    out_ref[...] = dot3(field_ref[...], mat_ref[0], NT)


def rest_kernel(field_ref, mat_ref, edge_ref, before_ref, out_ref, high_ref, low_ref):
    out_ref[...] = before_ref[...] + dot3(field_ref[...], mat_ref[0], NT)
    high_ref[...], low_ref[...] = halves(edge_ref[0])


def margin_product(a_ref, b_ref, high_ref, low_ref):
    dot = functools.partial(lax.dot_general, dimension_numbers=NT, preferred_element_type=F32)
    high, low = halves(jnp.concatenate(margins(a_ref, b_ref), axis=1))
    return dot(high, high_ref[...]) + (dot(low, high_ref[...]) + dot(high, low_ref[...]))


def local_kernel(a_ref, b_ref, own_ref, high_ref, low_ref, *refs):
    vecs, (out_ref, vecs_ref) = refs[:-2], refs[-2:]
    out_ref[...] = own_ref[...] + margin_product(a_ref, b_ref, high_ref, low_ref)
    for i, ref in enumerate(vecs):
        vecs_ref[i] = ref[0]


def solve_kernel(got_ref, one_ref, two_ref, local_ref, out_ref, beta_ref, wide_ref, *, total, maxev):
    nsub, pad, _ = got_ref.shape
    k = local_ref.shape[0]
    each = pad - 1
    nnar = one_ref.shape[0]
    ncol = LANES // k
    per = nsub // nnar
    chunk = per * each
    norms = jnp.sum(got_ref[:, pad - 1, :], axis=0, keepdims=True)
    beta = jnp.sqrt(as_col(norms, k) / total + EPS)
    res = got_ref[...].reshape(nsub * pad, LANES)
    wide_ref[...] = jnp.zeros_like(wide_ref)
    for c in range(nnar):
        for b in range(ncol):
            ref, at = (one_ref, b * chunk) if b < ncol // 2 else (two_ref, (b - ncol // 2) * chunk)
            piece = ref[c, at : at + chunk, :]
            for q in range(per):
                to = (c * per + q) * pad
                wide_ref[to : to + each, b * LANES : (b + 1) * LANES] = piece[q * each : (q + 1) * each]
    sol = dot3(res.T, wide_ref[...], NN)
    part = sum(sol[b * k : (b + 1) * k, b * LANES : (b + 1) * LANES] for b in range(ncol))
    both = jnp.concatenate([local_ref[...], part], axis=1) / beta
    for c in range(nnar):
        out_ref[c] = both
    beta_ref[...] = jnp.broadcast_to(beta, beta_ref.shape)


def precond_kernel(got_ref, lists_ref, count_ref, even_ref, odd_ref, own_ref, send_ref, mine_ref):
    n, k, width = got_ref.shape
    rdev = width - LANES
    maxev = even_ref.shape[1]
    nar = lax.axis_index("nar")
    sol = jnp.sum(got_ref[:, :, rdev:], axis=0)
    sol = jnp.where(iota(sol.shape, 1) < count_ref[0], sol, 0.0)[:, :maxev]
    for i in range(n):
        field = got_ref[nar ^ i, :, :rdev] + dot3(sol, (odd_ref if i % 2 else even_ref)[i // 2], NN)
        own_ref[:, pl.ds(pl.multiple_of((nar ^ i) * rdev, rdev), rdev)] = field
        if i == 0:
            mine_ref[...] = field
    ends = [
        exactly(pick_of(lists_ref[c, 4:5, :], rdev), own_ref[:, c * rdev : (c + 1) * rdev], NN, False)
        for c in range(n)
    ]
    weave(ends, send_ref)


def ratio(a, n):
    return jnp.where(n > 0, a / jnp.where(n > 0, n, 1.0), 0.0)


def image_kernel(a_ref, b_ref, own_ref, high_ref, low_ref, res_ref, beta_ref, image_ref, out_ref):
    k = own_ref.shape[0]
    image = own_ref[...] + margin_product(a_ref, b_ref, high_ref, low_ref)
    start = res_ref[:, 0, :] / beta_ref[:, :1]
    n = jnp.sum(start * start, axis=1, keepdims=True)
    a = jnp.sum(start * image, axis=1, keepdims=True)
    off = image - ratio(a, n) * start
    s = jnp.sum(off * off, axis=1, keepdims=True)
    image_ref[...] = image
    row = as_row(n) + pltpu.roll(as_row(a), k, 1) + pltpu.roll(as_row(s), 2 * k, 1)
    out_ref[...] = jnp.broadcast_to(row[None], out_ref.shape)


def end_kernel(got_ref, image_ref, res_ref, iter_ref, pre_ref, beta_ref, next_ref, new_ref, hess_ref, *, total):
    k = image_ref.shape[0]
    stats = got_ref[:, 0, :]
    n_i = stats
    a_i = pltpu.roll(stats, LANES - k, 1)
    s_i = pltpu.roll(stats, LANES - 2 * k, 1)
    n = jnp.sum(n_i, axis=0, keepdims=True)
    a = jnp.sum(a_i, axis=0, keepdims=True)
    h = ratio(a, n)
    gap = ratio(a_i, n_i) - h
    square = jnp.sum(s_i + (n_i * gap) * gap, axis=0, keepdims=True)
    beta = beta_ref[:, :1]
    lost = EPS / (beta * beta)
    a_col = as_col(a, k)
    h00 = a_col / total
    square = as_col(square, k) + a_col * as_col(h, k) * (lost * lost)
    h10 = jnp.sqrt(square / total + EPS)
    start = res_ref[:, 0, :] / beta
    next_ref[:, 0, :] = (image_ref[...] - h00 * start) / h10
    factor = beta * h00 / (h00 * h00 + h10 * h10)
    new_ref[:, 0, :] = iter_ref[:, 0, :] + factor * pre_ref[...]
    hess_ref[...] = jnp.concatenate([as_row(beta)[:, :k], as_row(h00)[:, :k], as_row(h10)[:, :k]], axis=0)


def exchange(blocks, axes):
    return lax.all_to_all(blocks, axes, 0, 0)


def beside(block, nsub, nnar):
    def partner(sub, nar):
        if nar % 2 == 0:
            return sub ^ 1
        return (sub + 1 if sub % 2 else sub - 1) % nsub

    route = [
        (sub * nnar + nar, partner(sub, nar) * nnar + nar) for sub in range(nsub) for nar in range(nnar)
    ]
    got = lax.ppermute(block, ("sub", "nar"), route)
    return got, across(got, nnar, 1)


def across(block, n, mask):
    return lax.ppermute(block, "nar", [(i, i ^ mask) for i in range(n)])


def product(field, matrix):
    rdev, ext = matrix.shape[1:]
    split = jax.ShapeDtypeStruct((rdev, ext - field.shape[1]), BF16)
    return local_call(product_kernel, (shape(field.shape[0], rdev), split, split), field, matrix, limit=10)


def product_in_two(field, matrix):
    k, own = field.shape
    rdev, ext = matrix.shape[1:]
    half = own // 2
    split = jax.ShapeDtypeStruct((rdev, ext - own), BF16)

    def columns(at):
        return pl.BlockSpec((1, rdev, half), lambda i: (0, 0, at))

    def rows(at):
        return pl.BlockSpec((k, half), lambda i: (0, at))

    first = local_call(
        half_kernel, shape(k, rdev), field, matrix, specs={0: rows(0), 1: columns(0)}, limit=8
    )
    return local_call(
        rest_kernel, (shape(k, rdev), split, split), field, matrix, matrix, first,
        specs={0: rows(1), 1: columns(1), 2: columns(2)}, limit=10,
    )


def per_device(
    residual, iterate, stiffness, local_inverse, eigvecs, ev_count, coarse_inverse, send_rows
):
    nsub, nnar = lax.axis_size("sub"), lax.axis_size("nar")
    k, _, rdev = residual.shape
    total = nsub * nnar * rdev
    over = send_rows.shape[2]
    maxev = eigvecs.shape[1]
    own = nnar * rdev
    ncol = LANES // k
    each = maxev // ncol // nnar
    pad = each + 1
    span = coarse_inverse.shape[1] // nnar
    head = rdev // LANES * k
    smem = pl.BlockSpec(memory_space=pltpu.SMEM)
    hbm = pl.BlockSpec(memory_space=pltpu.HBM)

    vecs = [eigvecs] + [across(eigvecs, nnar, m) for m in range(2, nnar, 2)]

    part = local_call(
        functools.partial(begin_kernel, each=each),
        shape(nnar, head + 8 + span, LANES), residual, eigvecs, coarse_inverse, send_rows, ev_count,
        specs={0: hbm, 1: hbm, 2: hbm, 3: hbm, 4: smem},
        scratch=[
            pltpu.VMEM((LANES, ncol * rdev), F32),
            pltpu.VMEM(residual.shape, F32),
            pltpu.VMEM(eigvecs.shape, F32),
            pltpu.VMEM(coarse_inverse.shape, F32),
            pltpu.VMEM(send_rows.shape, jnp.int32),
            pltpu.SemaphoreType.DMA((4,)),
        ],
        limit=62,
    )
    part = exchange(part, "nar")
    lists = pl.BlockSpec((nnar, 8, LANES), lambda i: (0, head // 8, 0))
    pieces = (shape(k, own), shape(k, nnar * over))
    res, r_own, send = local_call(
        middle_kernel, (shape(nsub, pad, LANES),) + pieces, part,
        specs={0: pl.BlockSpec((nnar, head + 8, LANES), lambda i: (0, 0, 0))},
    )
    res = exchange(res, "sub")

    got = beside(send, nsub, nnar)
    local, vecs = local_call(
        local_kernel, (shape(k, rdev), shape(nnar // 2, maxev, rdev)),
        *got, *product_in_two(r_own, local_inverse), *vecs,
    )
    vecs = (vecs, across(vecs, nnar, 1))

    first = (head + 8) // (span // 2)
    block, beta = local_call(
        functools.partial(solve_kernel, total=total, maxev=maxev),
        (shape(nnar, k, rdev + LANES), shape(k, LANES)), res, part, part, local,
        specs={
            j + 1: pl.BlockSpec((nnar, span // 2, LANES), lambda i, j=j: (0, first + j, 0))
            for j in range(2)
        },
        scratch=[pltpu.VMEM((nsub * pad, ncol * LANES), F32)],
    )
    block = exchange(block, "nar")
    p_own, send, precond = local_call(
        precond_kernel, pieces + (shape(k, rdev),), block, part, ev_count, *vecs,
        specs={1: lists, 2: smem},
    )

    got = beside(send, nsub, nnar)
    image, stats = local_call(
        image_kernel, (shape(k, rdev), shape(nsub * nnar, 1, LANES)),
        *got, *product_in_two(p_own, stiffness), residual, beta,
    )
    stats = exchange(stats, ("sub", "nar"))
    return local_call(
        functools.partial(end_kernel, total=total),
        (shape(k, 1, rdev), shape(k, 1, rdev), shape(3, k)),
        stats, image, residual, iterate, precond, beta,
    )


def solution(mesh):
    return jax.shard_map(
        per_device,
        mesh=mesh,
        in_specs=(
            P(None, "sub", "nar"),
            P(None, "sub", "nar"),
            P("sub", "nar", None),
            P("sub", "nar", None),
            P("sub", None, "nar"),
            P("sub"),
            P("sub", "nar"),
            P(None, "sub", "nar"),
        ),
        out_specs=(P(None, "sub", "nar"), P(None, "sub", "nar"), P()),
        check_vma=False,
    )
```

```python
import functools

import jax
import jax.numpy as jnp
from jax import lax
from jax.experimental import pallas as pl
from jax.experimental.pallas import tpu as pltpu
from jax.sharding import PartitionSpec as P

EPS = 1e-06
COSTS = {'middle_kernel': 0.01, 'product_kernel': 3, 'half_kernel': 1, 'rest_kernel': 1, 'local_kernel': 0.3, 'solve_kernel': 3, 'begin_kernel': 0.3, 'precond_kernel': 8}
F32, BF16 = jnp.float32, jnp.bfloat16
LANES = 128
NT = (((1,), (1,)), ((), ()))
NN = (((1,), (0,)), ((), ()))


def shape(*dims):
    return jax.ShapeDtypeStruct(dims, F32)


def whole(x):
    zeros = (0,) * len(x.shape)
    return pl.BlockSpec(x.shape, lambda i: zeros)


def local_call(body, outs, *args, specs=None, scratch=(), limit=6, cost=1):
    body_name = getattr(body, "func", body).__name__
    cost = COSTS.get(body_name, cost)
    many = isinstance(outs, tuple)
    specs = specs or {}
    return pl.pallas_call(
        body,
        grid=(1,),
        out_shape=outs,
        in_specs=[specs.get(i) or whole(x) for i, x in enumerate(args)],
        out_specs=tuple(whole(x) for x in outs) if many else whole(outs),
        scratch_shapes=scratch,
        compiler_params=pltpu.CompilerParams(vmem_limit_bytes=limit * 2**20),
        cost_estimate=pl.CostEstimate(flops=int(cost * 1e9), bytes_accessed=1024, transcendentals=0),
    )(*args)


def halves(x):
    high = x.astype(BF16)
    return high, (x - high.astype(F32)).astype(BF16)


def dot3(a, b, dims):
    dot = functools.partial(lax.dot_general, dimension_numbers=dims, preferred_element_type=F32)
    (ah, al), (bh, bl) = halves(a), halves(b)
    return dot(ah, bh) + (dot(al, bh) + dot(ah, bl))


def exactly(pick, x, dims, first):
    high = x.astype(BF16)
    rest = x - high.astype(F32)
    mid = rest.astype(BF16)
    low = (rest - mid.astype(F32)).astype(BF16)
    total = None
    for part in (low, mid, high):
        pair = (pick, part) if first else (part, pick)
        term = lax.dot_general(*pair, dimension_numbers=dims, preferred_element_type=F32)
        total = term if total is None else total + term
    return total


def iota(dims, axis):
    return lax.broadcasted_iota(jnp.int32, dims, axis)


def as_row(col):
    k = col.shape[0]
    return jnp.sum(jnp.where(iota((k, LANES), 0) == iota((k, LANES), 1), col, 0.0), axis=0, keepdims=True)


def as_col(row, k):
    return jnp.sum(jnp.where(iota((k, LANES), 0) == iota((k, LANES), 1), row, 0.0), axis=1, keepdims=True)


def own_list(rows_ref):
    even = lax.axis_index("sub") % 2 == 0
    rights, lefts = rows_ref[0], rows_ref[1]
    return jnp.concatenate([jnp.where(even, rights, lefts), jnp.where(even, lefts, rights)], axis=1)


def pick_of(listed, rdev):
    return (iota((rdev, LANES), 0).astype(F32) == listed).astype(F32).astype(BF16)


def masked(vecs_ref, count_ref):
    vecs = vecs_ref[0]
    return jnp.where(iota(vecs.shape, 0) < count_ref[0], vecs, 0.0)


def begin_kernel(
    res_hbm, vecs_hbm, inv_hbm, rows_hbm, count_ref, out_ref,
    wide_ref, res_ref, vecs_ref, inv_ref, rows_ref, sems, *, each
):
    pairs = ((res_hbm, res_ref), (vecs_hbm, vecs_ref), (inv_hbm, inv_ref), (rows_hbm, rows_ref))
    copies = [pltpu.make_async_copy(one, two, sems.at[i]) for i, (one, two) in enumerate(pairs)]
    for copy in copies:
        copy.start()
    wide_ref[...] = jnp.zeros_like(wide_ref)
    out_ref[...] = jnp.zeros_like(out_ref)
    for copy in copies:
        copy.wait()
    k, _, rdev = res_ref.shape
    r = res_ref[:, 0, :]
    vecs = masked(vecs_ref, count_ref)
    maxev = vecs.shape[0]
    ncol = LANES // k
    rows = maxev // ncol
    for b in range(ncol):
        wide_ref[b * k : (b + 1) * k, b * rdev : (b + 1) * rdev] = r
    left = jnp.concatenate([vecs[b * rows : (b + 1) * rows] for b in range(ncol)], axis=1)
    part = dot3(left, wide_ref[...], NT)
    norm = as_row(jnp.sum(r * r, axis=1, keepdims=True))
    listed = own_list(rows_ref).astype(F32)
    nnar = out_ref.shape[0]
    moved = coarse_columns(inv_ref[...], nnar=nnar, maxev=maxev, ncol=ncol, each=each)
    span = moved.shape[0] // nnar
    at = rdev // LANES * k
    for c in range(nnar):
        for i in range(rdev // LANES):
            out_ref[c, i * k : (i + 1) * k, :] = r[:, i * LANES : (i + 1) * LANES]
        out_ref[c, at : at + each, :] = part[c * each : (c + 1) * each]
        out_ref[c, at + each : at + each + 1, :] = norm
        out_ref[c, at + each + 1 : at + each + 2, :] = listed
        out_ref[c, at + 8 :, :maxev] = moved[c * span : (c + 1) * span]


def coarse_columns(inverse, *, nnar, maxev, ncol, each):
    ncols = inverse.shape[1]
    per = ncols // maxev
    p = iota((1, ncols), 1)
    a = p % each
    q = (p // each) % per
    b = (p // (each * per)) % ncol
    c = p // (each * per * ncol)
    want = q * maxev + b * (maxev // ncol) + c * each + a
    pick = (want == iota((ncols, ncols), 0)).astype(F32).astype(BF16)
    return exactly(pick, inverse, NN, False).T


def weave(ends, out_ref):
    half = LANES // 2
    core = lax.axis_index("nar") % 2
    low = iota(ends[0].shape, 1) < half
    for i in range(0, len(ends), 2):
        one, two = ends[i], ends[i + 1]
        first = jnp.where(low, one, pltpu.roll(two, half, 1))
        second = jnp.where(low, pltpu.roll(one, half, 1), two)
        out_ref[:, i * half : i * half + LANES] = jnp.where(core == 0, first, second)


def middle_kernel(got_ref, res_ref, own_ref, send_ref):
    n, _, lanes = got_ref.shape
    pad = res_ref.shape[1]
    k = own_ref.shape[0]
    rdev = own_ref.shape[1] // n
    halves_of = rdev // lanes
    at = halves_of * k
    total = jnp.sum(got_ref[:, at : at + 8, :], axis=0)[:pad]
    res_ref[...] = jnp.broadcast_to(total[None], res_ref.shape)
    ends = []
    for c in range(n):
        field = jnp.concatenate([got_ref[c, i * k : (i + 1) * k, :] for i in range(halves_of)], axis=1)
        own_ref[:, c * rdev : (c + 1) * rdev] = field
        listed = got_ref[c, at + 4 : at + 5, :]
        ends.append(exactly(pick_of(listed, rdev), field, NN, False))
    weave(ends, send_ref)


def margins(got_ref, other_ref):
    sub, nsub = lax.axis_index("sub"), lax.axis_size("sub")
    core = lax.axis_index("nar") % 2
    right = sub % 2 == core
    got, other = got_ref[...], other_ref[...]
    lefts = jnp.where(sub == 0, 0.0, jnp.where(right, other, got))
    rights = jnp.where(sub == nsub - 1, 0.0, jnp.where(right, got, other))
    return lefts, rights


def product_kernel(field_ref, mat_ref, out_ref, high_ref, low_ref):
    own = field_ref.shape[1]
    out_ref[...] = dot3(field_ref[...], mat_ref[0, :, :own], NT)
    high_ref[...], low_ref[...] = halves(mat_ref[0, :, own:])


def half_kernel(field_ref, mat_ref, out_ref):
    out_ref[...] = dot3(field_ref[...], mat_ref[0], NT)


def rest_kernel(field_ref, mat_ref, edge_ref, before_ref, out_ref, high_ref, low_ref):
    out_ref[...] = before_ref[...] + dot3(field_ref[...], mat_ref[0], NT)
    high_ref[...], low_ref[...] = halves(edge_ref[0])


def margin_product(a_ref, b_ref, high_ref, low_ref):
    dot = functools.partial(lax.dot_general, dimension_numbers=NT, preferred_element_type=F32)
    high, low = halves(jnp.concatenate(margins(a_ref, b_ref), axis=1))
    return dot(high, high_ref[...]) + (dot(low, high_ref[...]) + dot(high, low_ref[...]))


def local_kernel(a_ref, b_ref, own_ref, high_ref, low_ref, *refs):
    vecs, (out_ref, vecs_ref) = refs[:-2], refs[-2:]
    out_ref[...] = own_ref[...] + margin_product(a_ref, b_ref, high_ref, low_ref)
    for i, ref in enumerate(vecs):
        vecs_ref[i] = ref[0]


def solve_kernel(got_ref, one_ref, two_ref, local_ref, out_ref, beta_ref, wide_ref, *, total, maxev):
    nsub, pad, _ = got_ref.shape
    k = local_ref.shape[0]
    each = pad - 1
    nnar = one_ref.shape[0]
    ncol = LANES // k
    per = nsub // nnar
    chunk = per * each
    norms = jnp.sum(got_ref[:, pad - 1, :], axis=0, keepdims=True)
    beta = jnp.sqrt(as_col(norms, k) / total + EPS)
    res = got_ref[...].reshape(nsub * pad, LANES)
    wide_ref[...] = jnp.zeros_like(wide_ref)
    for c in range(nnar):
        for b in range(ncol):
            ref, at = (one_ref, b * chunk) if b < ncol // 2 else (two_ref, (b - ncol // 2) * chunk)
            piece = ref[c, at : at + chunk, :]
            for q in range(per):
                to = (c * per + q) * pad
                wide_ref[to : to + each, b * LANES : (b + 1) * LANES] = piece[q * each : (q + 1) * each]
    sol = dot3(res.T, wide_ref[...], NN)
    part = sum(sol[b * k : (b + 1) * k, b * LANES : (b + 1) * LANES] for b in range(ncol))
    both = jnp.concatenate([local_ref[...], part], axis=1) / beta
    for c in range(nnar):
        out_ref[c] = both
    beta_ref[...] = jnp.broadcast_to(beta, beta_ref.shape)


def precond_kernel(got_ref, lists_ref, count_ref, even_ref, odd_ref, own_ref, send_ref, mine_ref):
    n, k, width = got_ref.shape
    rdev = width - LANES
    maxev = even_ref.shape[1]
    nar = lax.axis_index("nar")
    sol = jnp.sum(got_ref[:, :, rdev:], axis=0)
    sol = jnp.where(iota(sol.shape, 1) < count_ref[0], sol, 0.0)[:, :maxev]
    for i in range(n):
        field = got_ref[nar ^ i, :, :rdev] + dot3(sol, (odd_ref if i % 2 else even_ref)[i // 2], NN)
        own_ref[:, pl.ds(pl.multiple_of((nar ^ i) * rdev, rdev), rdev)] = field
        if i == 0:
            mine_ref[...] = field
    ends = [
        exactly(pick_of(lists_ref[c, 4:5, :], rdev), own_ref[:, c * rdev : (c + 1) * rdev], NN, False)
        for c in range(n)
    ]
    weave(ends, send_ref)


def ratio(a, n):
    return jnp.where(n > 0, a / jnp.where(n > 0, n, 1.0), 0.0)


def image_kernel(a_ref, b_ref, own_ref, high_ref, low_ref, res_ref, beta_ref, image_ref, out_ref):
    k = own_ref.shape[0]
    image = own_ref[...] + margin_product(a_ref, b_ref, high_ref, low_ref)
    start = res_ref[:, 0, :] / beta_ref[:, :1]
    n = jnp.sum(start * start, axis=1, keepdims=True)
    a = jnp.sum(start * image, axis=1, keepdims=True)
    off = image - ratio(a, n) * start
    s = jnp.sum(off * off, axis=1, keepdims=True)
    image_ref[...] = image
    row = as_row(n) + pltpu.roll(as_row(a), k, 1) + pltpu.roll(as_row(s), 2 * k, 1)
    out_ref[...] = jnp.broadcast_to(row, out_ref.shape)


def end_kernel(got_ref, image_ref, res_ref, iter_ref, pre_ref, beta_ref, next_ref, new_ref, hess_ref, *, total):
    k = image_ref.shape[0]
    stats = got_ref[...]
    n_i = stats
    a_i = pltpu.roll(stats, LANES - k, 1)
    s_i = pltpu.roll(stats, LANES - 2 * k, 1)
    n = jnp.sum(n_i, axis=0, keepdims=True)
    a = jnp.sum(a_i, axis=0, keepdims=True)
    h = ratio(a, n)
    gap = ratio(a_i, n_i) - h
    square = jnp.sum(s_i + (n_i * gap) * gap, axis=0, keepdims=True)
    beta = beta_ref[:, :1]
    lost = EPS / (beta * beta)
    a_col = as_col(a, k)
    h00 = a_col / total
    square = as_col(square, k) + a_col * as_col(h, k) * (lost * lost)
    h10 = jnp.sqrt(square / total + EPS)
    start = res_ref[:, 0, :] / beta
    next_ref[:, 0, :] = (image_ref[...] - h00 * start) / h10
    factor = beta * h00 / (h00 * h00 + h10 * h10)
    new_ref[:, 0, :] = iter_ref[:, 0, :] + factor * pre_ref[...]
    hess_ref[...] = jnp.concatenate([as_row(beta)[:, :k], as_row(h00)[:, :k], as_row(h10)[:, :k]], axis=0)


def exchange(blocks, axes):
    return lax.all_to_all(blocks, axes, 0, 0)


def beside(block, nsub, nnar):
    def partner(sub, nar):
        if nar % 2 == 0:
            return sub ^ 1
        return (sub + 1 if sub % 2 else sub - 1) % nsub

    route = [
        (sub * nnar + nar, partner(sub, nar) * nnar + nar) for sub in range(nsub) for nar in range(nnar)
    ]
    got = lax.ppermute(block, ("sub", "nar"), route)
    return got, across(got, nnar, 1)


def across(block, n, mask):
    return lax.ppermute(block, "nar", [(i, i ^ mask) for i in range(n)])


def product(field, matrix):
    rdev, ext = matrix.shape[1:]
    split = jax.ShapeDtypeStruct((rdev, ext - field.shape[1]), BF16)
    return local_call(product_kernel, (shape(field.shape[0], rdev), split, split), field, matrix, limit=10)


def product_in_two(field, matrix):
    k, own = field.shape
    rdev, ext = matrix.shape[1:]
    half = own // 2
    split = jax.ShapeDtypeStruct((rdev, ext - own), BF16)

    def columns(at):
        return pl.BlockSpec((1, rdev, half), lambda i: (0, 0, at))

    def rows(at):
        return pl.BlockSpec((k, half), lambda i: (0, at))

    first = local_call(
        half_kernel, shape(k, rdev), field, matrix, specs={0: rows(0), 1: columns(0)}, limit=8
    )
    return local_call(
        rest_kernel, (shape(k, rdev), split, split), field, matrix, matrix, first,
        specs={0: rows(1), 1: columns(1), 2: columns(2)}, limit=10,
    )


def per_device(
    residual, iterate, stiffness, local_inverse, eigvecs, ev_count, coarse_inverse, send_rows
):
    nsub, nnar = lax.axis_size("sub"), lax.axis_size("nar")
    k, _, rdev = residual.shape
    total = nsub * nnar * rdev
    over = send_rows.shape[2]
    maxev = eigvecs.shape[1]
    own = nnar * rdev
    ncol = LANES // k
    each = maxev // ncol // nnar
    pad = each + 1
    span = coarse_inverse.shape[1] // nnar
    head = rdev // LANES * k
    smem = pl.BlockSpec(memory_space=pltpu.SMEM)
    hbm = pl.BlockSpec(memory_space=pltpu.HBM)

    vecs = [eigvecs] + [across(eigvecs, nnar, m) for m in range(2, nnar, 2)]

    part = local_call(
        functools.partial(begin_kernel, each=each),
        shape(nnar, head + 8 + span, LANES), residual, eigvecs, coarse_inverse, send_rows, ev_count,
        specs={0: hbm, 1: hbm, 2: hbm, 3: hbm, 4: smem},
        scratch=[
            pltpu.VMEM((LANES, ncol * rdev), F32),
            pltpu.VMEM(residual.shape, F32),
            pltpu.VMEM(eigvecs.shape, F32),
            pltpu.VMEM(coarse_inverse.shape, F32),
            pltpu.VMEM(send_rows.shape, jnp.int32),
            pltpu.SemaphoreType.DMA((4,)),
        ],
        limit=62,
    )
    part = exchange(part, "nar")
    lists = pl.BlockSpec((nnar, 8, LANES), lambda i: (0, head // 8, 0))
    pieces = (shape(k, own), shape(k, nnar * over))
    res, r_own, send = local_call(
        middle_kernel, (shape(nsub, pad, LANES),) + pieces, part,
        specs={0: pl.BlockSpec((nnar, head + 8, LANES), lambda i: (0, 0, 0))},
    )
    res = exchange(res, "sub")

    got = beside(send, nsub, nnar)
    local, vecs = local_call(
        local_kernel, (shape(k, rdev), shape(nnar // 2, maxev, rdev)),
        *got, *product_in_two(r_own, local_inverse), *vecs,
    )
    vecs = (vecs, across(vecs, nnar, 1))

    first = (head + 8) // (span // 2)
    block, beta = local_call(
        functools.partial(solve_kernel, total=total, maxev=maxev),
        (shape(nnar, k, rdev + LANES), shape(k, LANES)), res, part, part, local,
        specs={
            j + 1: pl.BlockSpec((nnar, span // 2, LANES), lambda i, j=j: (0, first + j, 0))
            for j in range(2)
        },
        scratch=[pltpu.VMEM((nsub * pad, ncol * LANES), F32)],
    )
    block = exchange(block, "nar")
    p_own, send, precond = local_call(
        precond_kernel, pieces + (shape(k, rdev),), block, part, ev_count, *vecs,
        specs={1: lists, 2: smem},
    )

    got = beside(send, nsub, nnar)
    image, stats = local_call(
        image_kernel, (shape(k, rdev), shape(nsub * nnar, LANES)),
        *got, *product_in_two(p_own, stiffness), residual, beta,
    )
    stats = exchange(stats[:, None], ("sub", "nar")).reshape(nsub * nnar, LANES)
    return local_call(
        functools.partial(end_kernel, total=total),
        (shape(k, 1, rdev), shape(k, 1, rdev), shape(3, k)),
        stats, image, residual, iterate, precond, beta,
    )


def solution(mesh):
    return jax.shard_map(
        per_device,
        mesh=mesh,
        in_specs=(
            P(None, "sub", "nar"),
            P(None, "sub", "nar"),
            P("sub", "nar", None),
            P("sub", "nar", None),
            P("sub", None, "nar"),
            P("sub"),
            P("sub", "nar"),
            P(None, "sub", "nar"),
        ),
        out_specs=(P(None, "sub", "nar"), P(None, "sub", "nar"), P()),
        check_vma=False,
    )
```

```python
import functools

import jax
import jax.numpy as jnp
from jax import lax
from jax.experimental import pallas as pl
from jax.experimental.pallas import tpu as pltpu
from jax.sharding import PartitionSpec as P

EPS = 1e-06
COSTS = {'middle_kernel': 0.01, 'product_kernel': 3, 'half_kernel': 1, 'rest_kernel': 1, 'local_kernel': 0.3, 'solve_kernel': 3, 'begin_kernel': 0.3, 'precond_kernel': 8}
F32, BF16 = jnp.float32, jnp.bfloat16
LANES = 128
NT = (((1,), (1,)), ((), ()))
NN = (((1,), (0,)), ((), ()))


def shape(*dims):
    return jax.ShapeDtypeStruct(dims, F32)


def whole(x):
    zeros = (0,) * len(x.shape)
    return pl.BlockSpec(x.shape, lambda i: zeros)


def local_call(body, outs, *args, specs=None, scratch=(), limit=6, cost=1):
    body_name = getattr(body, "func", body).__name__
    cost = COSTS.get(body_name, cost)
    many = isinstance(outs, tuple)
    specs = specs or {}
    return pl.pallas_call(
        body,
        grid=(1,),
        out_shape=outs,
        in_specs=[specs.get(i) or whole(x) for i, x in enumerate(args)],
        out_specs=tuple(whole(x) for x in outs) if many else whole(outs),
        scratch_shapes=scratch,
        compiler_params=pltpu.CompilerParams(vmem_limit_bytes=limit * 2**20),
        cost_estimate=pl.CostEstimate(flops=int(cost * 1e9), bytes_accessed=1024, transcendentals=0),
    )(*args)


def halves(x):
    high = x.astype(BF16)
    return high, (x - high.astype(F32)).astype(BF16)


def stacked(parts):
    return jnp.concatenate(parts, axis=0).astype(BF16)


def dot3(a, b, dims):
    dot = functools.partial(lax.dot_general, dimension_numbers=dims, preferred_element_type=F32)
    rows = a.shape[0]
    high = a.astype(BF16).astype(F32)
    bh, bl = halves(b)
    both = dot(stacked([high, a - high]), bh)
    return both[:rows] + (both[rows:] + dot(high.astype(BF16), bl))


def exactly(pick, x, dims):
    rows = x.shape[0]
    high = x.astype(BF16).astype(F32)
    rest = x - high
    mid = rest.astype(BF16).astype(F32)
    out = lax.dot_general(
        stacked([rest - mid, mid, high]), pick, dimension_numbers=dims, preferred_element_type=F32
    )
    return out[:rows] + out[rows : 2 * rows] + out[2 * rows :]


def iota(dims, axis):
    return lax.broadcasted_iota(jnp.int32, dims, axis)


def as_row(col):
    k = col.shape[0]
    return jnp.sum(jnp.where(iota((k, LANES), 0) == iota((k, LANES), 1), col, 0.0), axis=0, keepdims=True)


def as_col(row, k):
    return jnp.sum(jnp.where(iota((k, LANES), 0) == iota((k, LANES), 1), row, 0.0), axis=1, keepdims=True)


def own_list(rows_ref):
    even = lax.axis_index("sub") % 2 == 0
    rights, lefts = rows_ref[0], rows_ref[1]
    return jnp.concatenate([jnp.where(even, rights, lefts), jnp.where(even, lefts, rights)], axis=1)


def pick_of(listed, rdev):
    return (iota((rdev, LANES), 0).astype(F32) == listed).astype(F32).astype(BF16)


def masked(vecs_ref, count_ref):
    vecs = vecs_ref[0]
    return jnp.where(iota(vecs.shape, 0) < count_ref[0], vecs, 0.0)


def begin_kernel(
    res_hbm, vecs_hbm, inv_hbm, rows_hbm, count_ref, out_ref,
    wide_ref, res_ref, vecs_ref, inv_ref, rows_ref, sems, *, each
):
    pairs = ((res_hbm, res_ref), (vecs_hbm, vecs_ref), (inv_hbm, inv_ref), (rows_hbm, rows_ref))
    copies = [pltpu.make_async_copy(one, two, sems.at[i]) for i, (one, two) in enumerate(pairs)]
    for copy in copies:
        copy.start()
    wide_ref[...] = jnp.zeros_like(wide_ref)
    out_ref[...] = jnp.zeros_like(out_ref)
    for copy in copies:
        copy.wait()
    k, _, rdev = res_ref.shape
    r = res_ref[:, 0, :]
    vecs = masked(vecs_ref, count_ref)
    maxev = vecs.shape[0]
    ncol = LANES // k
    rows = maxev // ncol
    for b in range(ncol):
        wide_ref[b * k : (b + 1) * k, b * rdev : (b + 1) * rdev] = r
    left = jnp.concatenate([vecs[b * rows : (b + 1) * rows] for b in range(ncol)], axis=1)
    part = dot3(left, wide_ref[...], NT)
    norm = as_row(jnp.sum(r * r, axis=1, keepdims=True))
    listed = own_list(rows_ref).astype(F32)
    nnar = out_ref.shape[0]
    moved = coarse_columns(inv_ref[...], nnar=nnar, maxev=maxev, ncol=ncol, each=each)
    span = moved.shape[0] // nnar
    at = rdev // LANES * k
    for c in range(nnar):
        for i in range(rdev // LANES):
            out_ref[c, i * k : (i + 1) * k, :] = r[:, i * LANES : (i + 1) * LANES]
        out_ref[c, at : at + each, :] = part[c * each : (c + 1) * each]
        out_ref[c, at + each : at + each + 1, :] = norm
        out_ref[c, at + each + 1 : at + each + 2, :] = listed
        out_ref[c, at + 8 :, :maxev] = moved[c * span : (c + 1) * span]


def coarse_columns(inverse, *, nnar, maxev, ncol, each):
    ncols = inverse.shape[1]
    per = ncols // maxev
    p = iota((1, ncols), 1)
    a = p % each
    q = (p // each) % per
    b = (p // (each * per)) % ncol
    c = p // (each * per * ncol)
    want = q * maxev + b * (maxev // ncol) + c * each + a
    pick = (want == iota((ncols, ncols), 0)).astype(F32).astype(BF16)
    return exactly(pick, inverse, NN).T


def weave(ends, out_ref):
    half = LANES // 2
    core = lax.axis_index("nar") % 2
    low = iota(ends[0].shape, 1) < half
    for i in range(0, len(ends), 2):
        one, two = ends[i], ends[i + 1]
        first = jnp.where(low, one, pltpu.roll(two, half, 1))
        second = jnp.where(low, pltpu.roll(one, half, 1), two)
        out_ref[:, i * half : i * half + LANES] = jnp.where(core == 0, first, second)


def middle_kernel(got_ref, res_ref, own_ref, send_ref):
    n, _, lanes = got_ref.shape
    pad = res_ref.shape[1]
    k = own_ref.shape[0]
    rdev = own_ref.shape[1] // n
    halves_of = rdev // lanes
    at = halves_of * k
    total = jnp.sum(got_ref[:, at : at + 8, :], axis=0)[:pad]
    res_ref[...] = jnp.broadcast_to(total[None], res_ref.shape)
    ends = []
    for c in range(n):
        field = jnp.concatenate([got_ref[c, i * k : (i + 1) * k, :] for i in range(halves_of)], axis=1)
        own_ref[:, c * rdev : (c + 1) * rdev] = field
        listed = got_ref[c, at + 4 : at + 5, :]
        ends.append(exactly(pick_of(listed, rdev), field, NN))
    weave(ends, send_ref)


def margins(got_ref, other_ref):
    sub, nsub = lax.axis_index("sub"), lax.axis_size("sub")
    core = lax.axis_index("nar") % 2
    right = sub % 2 == core
    got, other = got_ref[...], other_ref[...]
    lefts = jnp.where(sub == 0, 0.0, jnp.where(right, other, got))
    rights = jnp.where(sub == nsub - 1, 0.0, jnp.where(right, got, other))
    return lefts, rights


def product_kernel(field_ref, mat_ref, out_ref, high_ref, low_ref):
    own = field_ref.shape[1]
    out_ref[...] = dot3(field_ref[...], mat_ref[0, :, :own], NT)
    high_ref[...], low_ref[...] = halves(mat_ref[0, :, own:])


def half_kernel(field_ref, mat_ref, out_ref):
    out_ref[...] = dot3(field_ref[...], mat_ref[0], NT)


def rest_kernel(field_ref, mat_ref, edge_ref, before_ref, out_ref, high_ref, low_ref):
    out_ref[...] = before_ref[...] + dot3(field_ref[...], mat_ref[0], NT)
    high_ref[...], low_ref[...] = halves(edge_ref[0])


def margin_product(a_ref, b_ref, high_ref, low_ref):
    dot = functools.partial(lax.dot_general, dimension_numbers=NT, preferred_element_type=F32)
    field = jnp.concatenate(margins(a_ref, b_ref), axis=1)
    rows = field.shape[0]
    high = field.astype(BF16).astype(F32)
    both = dot(stacked([high, field - high]), high_ref[...])
    return both[:rows] + (both[rows:] + dot(high.astype(BF16), low_ref[...]))


def local_kernel(a_ref, b_ref, own_ref, high_ref, low_ref, *refs):
    vecs, (out_ref, vecs_ref) = refs[:-2], refs[-2:]
    out_ref[...] = own_ref[...] + margin_product(a_ref, b_ref, high_ref, low_ref)
    for i, ref in enumerate(vecs):
        vecs_ref[i] = ref[0]


def solve_kernel(got_ref, one_ref, two_ref, local_ref, out_ref, beta_ref, wide_ref, *, total, maxev):
    nsub, pad, _ = got_ref.shape
    k = local_ref.shape[0]
    each = pad - 1
    nnar = one_ref.shape[0]
    ncol = LANES // k
    per = nsub // nnar
    chunk = per * each
    norms = jnp.sum(got_ref[:, pad - 1, :], axis=0, keepdims=True)
    beta = jnp.sqrt(as_col(norms, k) / total + EPS)
    res = got_ref[...].reshape(nsub * pad, LANES)
    wide_ref[...] = jnp.zeros_like(wide_ref)
    for c in range(nnar):
        for b in range(ncol):
            ref, at = (one_ref, b * chunk) if b < ncol // 2 else (two_ref, (b - ncol // 2) * chunk)
            piece = ref[c, at : at + chunk, :]
            for q in range(per):
                to = (c * per + q) * pad
                wide_ref[to : to + each, b * LANES : (b + 1) * LANES] = piece[q * each : (q + 1) * each]
    sol = dot3(res.T, wide_ref[...], NN)
    part = sum(sol[b * k : (b + 1) * k, b * LANES : (b + 1) * LANES] for b in range(ncol))
    both = jnp.concatenate([local_ref[...], part], axis=1) / beta
    for c in range(nnar):
        out_ref[c] = both
    beta_ref[...] = jnp.broadcast_to(beta, beta_ref.shape)


def precond_kernel(got_ref, lists_ref, count_ref, even_ref, odd_ref, own_ref, send_ref, mine_ref):
    n, k, width = got_ref.shape
    rdev = width - LANES
    maxev = even_ref.shape[1]
    nar = lax.axis_index("nar")
    sol = jnp.sum(got_ref[:, :, rdev:], axis=0)
    sol = jnp.where(iota(sol.shape, 1) < count_ref[0], sol, 0.0)[:, :maxev]
    for i in range(n):
        field = got_ref[nar ^ i, :, :rdev] + dot3(sol, (odd_ref if i % 2 else even_ref)[i // 2], NN)
        own_ref[:, pl.ds(pl.multiple_of((nar ^ i) * rdev, rdev), rdev)] = field
        if i == 0:
            mine_ref[...] = field
    ends = [
        exactly(pick_of(lists_ref[c, 4:5, :], rdev), own_ref[:, c * rdev : (c + 1) * rdev], NN)
        for c in range(n)
    ]
    weave(ends, send_ref)


def ratio(a, n):
    return jnp.where(n > 0, a / jnp.where(n > 0, n, 1.0), 0.0)


def image_kernel(a_ref, b_ref, own_ref, high_ref, low_ref, res_ref, beta_ref, image_ref, out_ref):
    k = own_ref.shape[0]
    image = own_ref[...] + margin_product(a_ref, b_ref, high_ref, low_ref)
    start = res_ref[:, 0, :] / beta_ref[:, :1]
    n = jnp.sum(start * start, axis=1, keepdims=True)
    a = jnp.sum(start * image, axis=1, keepdims=True)
    off = image - ratio(a, n) * start
    s = jnp.sum(off * off, axis=1, keepdims=True)
    image_ref[...] = image
    row = as_row(n) + pltpu.roll(as_row(a), k, 1) + pltpu.roll(as_row(s), 2 * k, 1)
    out_ref[...] = jnp.broadcast_to(row, out_ref.shape)


def end_kernel(got_ref, image_ref, res_ref, iter_ref, pre_ref, beta_ref, next_ref, new_ref, hess_ref, *, total):
    k = image_ref.shape[0]
    stats = got_ref[...]
    n_i = stats
    a_i = pltpu.roll(stats, LANES - k, 1)
    s_i = pltpu.roll(stats, LANES - 2 * k, 1)
    n = jnp.sum(n_i, axis=0, keepdims=True)
    a = jnp.sum(a_i, axis=0, keepdims=True)
    h = ratio(a, n)
    gap = ratio(a_i, n_i) - h
    square = jnp.sum(s_i + (n_i * gap) * gap, axis=0, keepdims=True)
    beta = beta_ref[:, :1]
    lost = EPS / (beta * beta)
    a_col = as_col(a, k)
    h00 = a_col / total
    square = as_col(square, k) + a_col * as_col(h, k) * (lost * lost)
    h10 = jnp.sqrt(square / total + EPS)
    start = res_ref[:, 0, :] / beta
    next_ref[:, 0, :] = (image_ref[...] - h00 * start) / h10
    factor = beta * h00 / (h00 * h00 + h10 * h10)
    new_ref[:, 0, :] = iter_ref[:, 0, :] + factor * pre_ref[...]
    hess_ref[...] = jnp.concatenate([as_row(beta)[:, :k], as_row(h00)[:, :k], as_row(h10)[:, :k]], axis=0)


def exchange(blocks, axes):
    return lax.all_to_all(blocks, axes, 0, 0)


def beside(block, nsub, nnar):
    def partner(sub, nar):
        if nar % 2 == 0:
            return sub ^ 1
        return (sub + 1 if sub % 2 else sub - 1) % nsub

    route = [
        (sub * nnar + nar, partner(sub, nar) * nnar + nar) for sub in range(nsub) for nar in range(nnar)
    ]
    got = lax.ppermute(block, ("sub", "nar"), route)
    return got, across(got, nnar, 1)


def across(block, n, mask):
    return lax.ppermute(block, "nar", [(i, i ^ mask) for i in range(n)])


def product(field, matrix):
    rdev, ext = matrix.shape[1:]
    split = jax.ShapeDtypeStruct((rdev, ext - field.shape[1]), BF16)
    return local_call(product_kernel, (shape(field.shape[0], rdev), split, split), field, matrix, limit=10)


def product_in_two(field, matrix):
    k, own = field.shape
    rdev, ext = matrix.shape[1:]
    half = own // 2
    split = jax.ShapeDtypeStruct((rdev, ext - own), BF16)

    def columns(at):
        return pl.BlockSpec((1, rdev, half), lambda i: (0, 0, at))

    def rows(at):
        return pl.BlockSpec((k, half), lambda i: (0, at))

    first = local_call(
        half_kernel, shape(k, rdev), field, matrix, specs={0: rows(0), 1: columns(0)}, limit=8
    )
    return local_call(
        rest_kernel, (shape(k, rdev), split, split), field, matrix, matrix, first,
        specs={0: rows(1), 1: columns(1), 2: columns(2)}, limit=10,
    )


def per_device(
    residual, iterate, stiffness, local_inverse, eigvecs, ev_count, coarse_inverse, send_rows
):
    nsub, nnar = lax.axis_size("sub"), lax.axis_size("nar")
    k, _, rdev = residual.shape
    total = nsub * nnar * rdev
    over = send_rows.shape[2]
    maxev = eigvecs.shape[1]
    own = nnar * rdev
    ncol = LANES // k
    each = maxev // ncol // nnar
    pad = each + 1
    span = coarse_inverse.shape[1] // nnar
    head = rdev // LANES * k
    smem = pl.BlockSpec(memory_space=pltpu.SMEM)
    hbm = pl.BlockSpec(memory_space=pltpu.HBM)

    vecs = [eigvecs] + [across(eigvecs, nnar, m) for m in range(2, nnar, 2)]

    part = local_call(
        functools.partial(begin_kernel, each=each),
        shape(nnar, head + 8 + span, LANES), residual, eigvecs, coarse_inverse, send_rows, ev_count,
        specs={0: hbm, 1: hbm, 2: hbm, 3: hbm, 4: smem},
        scratch=[
            pltpu.VMEM((LANES, ncol * rdev), F32),
            pltpu.VMEM(residual.shape, F32),
            pltpu.VMEM(eigvecs.shape, F32),
            pltpu.VMEM(coarse_inverse.shape, F32),
            pltpu.VMEM(send_rows.shape, jnp.int32),
            pltpu.SemaphoreType.DMA((4,)),
        ],
        limit=62,
    )
    part = exchange(part, "nar")
    lists = pl.BlockSpec((nnar, 8, LANES), lambda i: (0, head // 8, 0))
    pieces = (shape(k, own), shape(k, nnar * over))
    res, r_own, send = local_call(
        middle_kernel, (shape(nsub, pad, LANES),) + pieces, part,
        specs={0: pl.BlockSpec((nnar, head + 8, LANES), lambda i: (0, 0, 0))},
    )
    res = exchange(res, "sub")

    got = beside(send, nsub, nnar)
    local, vecs = local_call(
        local_kernel, (shape(k, rdev), shape(nnar // 2, maxev, rdev)),
        *got, *product_in_two(r_own, local_inverse), *vecs,
    )
    vecs = (vecs, across(vecs, nnar, 1))

    first = (head + 8) // (span // 2)
    block, beta = local_call(
        functools.partial(solve_kernel, total=total, maxev=maxev),
        (shape(nnar, k, rdev + LANES), shape(k, LANES)), res, part, part, local,
        specs={
            j + 1: pl.BlockSpec((nnar, span // 2, LANES), lambda i, j=j: (0, first + j, 0))
            for j in range(2)
        },
        scratch=[pltpu.VMEM((nsub * pad, ncol * LANES), F32)],
    )
    block = exchange(block, "nar")
    p_own, send, precond = local_call(
        precond_kernel, pieces + (shape(k, rdev),), block, part, ev_count, *vecs,
        specs={1: lists, 2: smem},
    )

    got = beside(send, nsub, nnar)
    image, stats = local_call(
        image_kernel, (shape(k, rdev), shape(nsub * nnar, LANES)),
        *got, *product_in_two(p_own, stiffness), residual, beta,
    )
    stats = exchange(stats[:, None], ("sub", "nar")).reshape(nsub * nnar, LANES)
    return local_call(
        functools.partial(end_kernel, total=total),
        (shape(k, 1, rdev), shape(k, 1, rdev), shape(3, k)),
        stats, image, residual, iterate, precond, beta,
    )


def solution(mesh):
    return jax.shard_map(
        per_device,
        mesh=mesh,
        in_specs=(
            P(None, "sub", "nar"),
            P(None, "sub", "nar"),
            P("sub", "nar", None),
            P("sub", "nar", None),
            P("sub", None, "nar"),
            P("sub"),
            P("sub", "nar"),
            P(None, "sub", "nar"),
        ),
        out_specs=(P(None, "sub", "nar"), P(None, "sub", "nar"), P()),
        check_vma=False,
    )
```
